512 devices in a mesh: row: 32 (over y, x), col: 16 (over z, core).
Axes of the slice: x: 4, y: 8, z: 8, core: 2. Of those that a mesh axis runs over, the one named last changes fastest.
Arguments:
- tokens: bfloat16 [2048, 4096], P('col', 'row'), may hold values from -6 to 6
- gate_weight: bfloat16 [4096, 16384], P('col', 'row'), may hold values from -0.09375 to 0.09375
- up_weight: bfloat16 [4096, 16384], P('col', 'row'), may hold values from -0.09375 to 0.09375
- gate_keep: int32 [32, 128], P('col', 'row'), may hold values from 0 to 1, as said below
- up_keep: int32 [32, 128], P('col', 'row'), may hold values from 0 to 1, as said below
- cotangent: bfloat16 [2048, 16384], P('col', 'row'), may hold values from -1.5 to 1.5
Outputs:
- hidden: bfloat16 [2048, 16384], P('col', 'row')
- grad_tokens: bfloat16 [2048, 4096], P('row', 'col')
- grad_gate: float32 [4096, 16384], P('col', 'row')
- grad_up: float32 [4096, 16384], P('col', 'row')
The draws below stay inside these ranges and needn't reach their ends.
Inputs may be any that keep to these rules, and one draw needn't show every extreme that they name: `gate_keep`: 1 keeps a tile of 128 x 128 weights, 0 prunes it; in every tile column, each aligned group of 2 tile rows keeps exactly 1 tiles. `up_keep`: 1 keeps a tile of 128 x 128 weights, 0 prunes it; in every tile column, each aligned group of 2 tile rows keeps exactly 1 tiles.
All inputs are finite; a program needn't handle non-finite values.
Results may differ from the reference program's by a relative error of at most 0.0049.
Values may be sent and summed in bfloat16 or wider, within the bound.
No kernel may reach another device: no remote copies, remote signals or barrier semaphores. Data moves between devices by JAX's collectives and lax.ppermute only.
A program may use at most 64 MiB of HBM per device.

```python
import jax
import jax.numpy as jnp
from jax import lax

D = 4096
F = 16384
BLOCK = 128
TOKENS = 2048
TILE_ROWS = 2
KEEP = 1


def kept_tiles(key):
    groups = D // BLOCK // TILE_ROWS
    columns = F // BLOCK
    scores = jax.random.randint(key, (groups, TILE_ROWS, columns), 0, 1 << 20)
    scores = scores * TILE_ROWS + jnp.arange(TILE_ROWS, dtype=jnp.int32)[None, :, None]
    ranking = jnp.argsort(jnp.argsort(scores, axis=1, stable=True), axis=1, stable=True)
    return (ranking < KEEP).astype(jnp.int32).reshape(D // BLOCK, columns)


def draw_gate_keep(key, part):
    key = jax.random.fold_in(key, 3)
    return kept_tiles(key)


def draw_up_keep(key, part):
    key = jax.random.fold_in(key, 7)
    return kept_tiles(key)


def steps_of(key, shape, cuts, smallest, high):
    loudness = 1.0
    for position, parts in cuts:
        draws = jax.random.uniform(jax.random.fold_in(jax.random.fold_in(key, 6), position), (parts,), jnp.float32, smallest / len(cuts), high / len(cuts))
        loudness = loudness * jnp.repeat(jnp.exp(draws), shape[position] // parts).reshape((-1,) + (1,) * (len(shape) - 1 - position))
    return loudness


def scatter_about(rng, dims, deviation, bound, cuts=(), held_as=jnp.bfloat16):
    values = jax.random.normal(rng, dims, jnp.float32) * deviation
    if len(cuts) > 0:
        values = steps_of(rng, dims, cuts, -0.22, 0.18) * values
    return jnp.clip(values, min=-bound, max=bound).astype(held_as)


def setup_inputs(seed: int = 0) -> dict:
    arg_keys = jax.random.split(jax.random.key(seed), 7)
    return {
        "tokens": scatter_about(arg_keys[0], (TOKENS, D), 1.0, 6.0, ((0, 16), (1, 32))),
        "gate_weight": scatter_about(arg_keys[1], (D, F), D ** -0.5, 0.09375, ((0, 16), (1, 32))),
        "up_weight": scatter_about(arg_keys[2], (D, F), D ** -0.5, 0.09375, ((0, 16), (1, 32))),
        "gate_keep": draw_gate_keep(jax.random.fold_in(arg_keys[6], 71), 0),
        "up_keep": draw_up_keep(jax.random.fold_in(arg_keys[6], 71), 0),
        "cotangent": scatter_about(arg_keys[5], (TOKENS, F), 0.25, 1.5, ((0, 16), (1, 32))),
    }


def spread(tile_keep):
    return jnp.repeat(jnp.repeat(tile_keep, BLOCK, 0), BLOCK, 1).astype(jnp.bfloat16)


def reference(tokens, gate_weight, up_weight, gate_keep, up_keep, cotangent):
    gate_mask = spread(gate_keep)
    up_mask = spread(up_keep)
    pruned_gate = gate_weight * gate_mask
    pruned_up = up_weight * up_mask
    gate = jnp.dot(tokens, pruned_gate, preferred_element_type=jnp.float32)
    up = jnp.dot(tokens, pruned_up, preferred_element_type=jnp.float32)
    sigmoid_gate = jax.nn.sigmoid(gate)
    activated = gate * sigmoid_gate
    hidden = (activated * up).astype(jnp.bfloat16)
    grad_out = cotangent.astype(jnp.float32)
    d_gate = (grad_out * up * sigmoid_gate * (1.0 + gate * (1.0 - sigmoid_gate))).astype(jnp.bfloat16)
    d_up = (grad_out * activated).astype(jnp.bfloat16)
    contract_last = (((1,), (1,)), ((), ()))
    grad_tokens = lax.dot_general(d_gate, pruned_gate, contract_last, preferred_element_type=jnp.float32)
    grad_tokens = grad_tokens + lax.dot_general(d_up, pruned_up, contract_last, preferred_element_type=jnp.float32)
    contract_first = (((0,), (0,)), ((), ()))
    grad_gate = lax.dot_general(tokens, d_gate, contract_first, preferred_element_type=jnp.float32) * gate_mask.astype(jnp.float32)
    grad_up = lax.dot_general(tokens, d_up, contract_first, preferred_element_type=jnp.float32) * up_mask.astype(jnp.float32)
    return hidden, grad_tokens.astype(jnp.bfloat16), grad_gate, grad_up
```

```python
import jax
import jax.numpy as jnp
from jax import lax
from jax.sharding import PartitionSpec as P

BLOCK = 128
bf16 = jnp.bfloat16
f32 = jnp.float32


def kept(weight, keep):
    first = jnp.repeat(keep[0], BLOCK)[None, :] > 0
    return jnp.where(first, weight[:BLOCK], weight[BLOCK:]), first.astype(bf16)


def shards(tokens, gate_weight, up_weight, gate_keep, up_keep, cotangent):
    rows, cols = lax.axis_size("row"), lax.axis_size("col")
    count, width = tokens.shape
    units = cotangent.shape[1]

    gate_tile, gate_first = kept(gate_weight, gate_keep)
    up_tile, up_first = kept(up_weight, up_keep)
    packed = jnp.concatenate(
        [
            gate_tile,
            up_tile,
            jnp.broadcast_to(gate_first, (8, units)),
            jnp.broadcast_to(up_first, (8, units)),
        ],
        axis=0,
    )
    weights = lax.all_gather(packed, "col", axis=0)

    copies = jnp.broadcast_to(tokens[None], (rows, count, width))
    blocks = lax.all_to_all(copies, "row", 0, 0, tiled=True)
    rows_full = blocks.transpose(1, 0, 2).reshape(count, rows * width)

    def spread(tile, first):
        both = jnp.stack([tile * first, tile * (1 - first)], axis=1)
        return both.reshape(cols * 2 * BLOCK, units)

    pruned_gate = spread(weights[:, :BLOCK], weights[:, 2 * BLOCK : 2 * BLOCK + 1])
    pruned_up = spread(weights[:, BLOCK : 2 * BLOCK], weights[:, 2 * BLOCK + 8 : 2 * BLOCK + 9])

    gate = jnp.dot(rows_full, pruned_gate, preferred_element_type=f32)
    up = jnp.dot(rows_full, pruned_up, preferred_element_type=f32)
    sigmoid_gate = jax.nn.sigmoid(gate)
    activated = gate * sigmoid_gate
    hidden = (activated * up).astype(bf16)
    grad_out = cotangent.astype(f32)
    d_gate = (grad_out * up * sigmoid_gate * (1.0 + gate * (1.0 - sigmoid_gate))).astype(bf16)
    d_up = (grad_out * activated).astype(bf16)

    both_all = lax.all_gather(jnp.concatenate([d_gate, d_up], axis=1), "col", axis=0, tiled=True)

    contract_last = (((1,), (1,)), ((), ()))
    share = lax.dot_general(
        d_gate, pruned_gate, contract_last, preferred_element_type=f32
    ) + lax.dot_general(d_up, pruned_up, contract_last, preferred_element_type=f32)
    share = share.astype(bf16).reshape(count, rows, width).transpose(1, 0, 2)
    shares = lax.all_to_all(share, "row", 0, 0, tiled=True)
    total = jnp.sum(shares.astype(f32), axis=0).astype(bf16)
    row = lax.axis_index("row")
    half = count // 2
    odd = row % 2
    pieces = []
    for flip in range(2):
        route = []
        for r in range(rows):
            for c in range(cols):
                to = (2 * c + ((r % 2) ^ flip)) * cols + r // 2
                route.append((r * cols + c, to))
        piece = jnp.where((odd ^ flip) == 1, total[half:], total[:half])
        pieces.append(lax.ppermute(piece, ("row", "col"), route))
    left = jnp.where(odd == 0, pieces[0], pieces[1])
    right = jnp.where(odd == 0, pieces[1], pieces[0])
    grad_tokens = jnp.concatenate([left, right], axis=1)

    by_col = blocks.reshape(cols, rows // cols, count, width)
    columns = lax.all_to_all(by_col, "col", 0, 0, tiled=True)
    columns = columns.transpose(0, 2, 1, 3).reshape(cols * count, (rows // cols) * width)
    grads = lax.dot_general(
        columns, both_all, (((0,), (0,)), ((), ())), preferred_element_type=f32
    )
    gate_mask = jnp.repeat(jnp.repeat(gate_keep, BLOCK, 0), BLOCK, 1).astype(f32)
    up_mask = jnp.repeat(jnp.repeat(up_keep, BLOCK, 0), BLOCK, 1).astype(f32)
    return hidden, grad_tokens, grads[:, :units] * gate_mask, grads[:, units:] * up_mask


def solution(mesh):
    return jax.shard_map(
        shards,
        mesh=mesh,
        in_specs=(P("col", "row"),) * 6,
        out_specs=(P("col", "row"), P("row", "col"), P("col", "row"), P("col", "row")),
        check_vma=False,
    )
```

```python
import jax
import jax.numpy as jnp
from jax import lax
from jax.experimental import pallas as pl
from jax.experimental.pallas import tpu as pltpu
from jax.sharding import PartitionSpec as P

BLOCK = 128
EXTRA = 16
bf16 = jnp.bfloat16
f16 = jnp.float16
f32 = jnp.float32


def exponent(largest):
    return jnp.floor(14.0 - jnp.log2(jnp.maximum(largest, 2.0**-100)))


def kept(weight, first):
    return jnp.where(first, weight[:BLOCK], weight[BLOCK:]).astype(f32)


def forward(x_ref, w_ref, grad_ref, hidden_ref, both_ref, share_ref, rows, full):
    groups, units = w_ref.shape[0], w_ref.shape[2]
    for tile in range(x_ref.shape[0]):
        rows[:, tile * BLOCK : (tile + 1) * BLOCK] = x_ref[tile]

    def expand(g, carry):
        at = pl.ds(pl.multiple_of(g * 2 * BLOCK, BLOCK), BLOCK)
        after = pl.ds(pl.multiple_of(g * 2 * BLOCK + BLOCK, BLOCK), BLOCK)
        marks = w_ref[g, 2 * BLOCK : 2 * BLOCK + EXTRA, :]
        for part in range(2):
            columns = pl.ds(part * units, units)
            tile = w_ref[g, part * BLOCK : (part + 1) * BLOCK, :]
            first = marks[part : part + 1]
            full[at, columns] = tile * first
            full[after, columns] = tile * (1 - first)
        return carry

    lax.fori_loop(0, groups, expand, 0)
    step = 256
    for n in range(0, units, step):
        gate = jnp.dot(rows[...], full[:, n : n + step], preferred_element_type=f32)
        up = jnp.dot(rows[...], full[:, units + n : units + n + step], preferred_element_type=f32)
        sigmoid_gate = jax.nn.sigmoid(gate)
        activated = gate * sigmoid_gate
        hidden_ref[:, n : n + step] = (activated * up).astype(bf16)
        grad_out = grad_ref[:, n : n + step].astype(f32)
        d_gate = grad_out * up * sigmoid_gate * (1.0 + gate * (1.0 - sigmoid_gate))
        both_ref[:, n : n + step] = d_gate.astype(bf16)
        both_ref[:, units + n : units + n + step] = (grad_out * activated).astype(bf16)

    def back(g, carry):
        at = pl.ds(pl.multiple_of(g * 2 * BLOCK, BLOCK), 2 * BLOCK)
        pair = lax.dot_general(
            both_ref[...], full[at, :], (((1,), (1,)), ((), ())), preferred_element_type=f32
        ).astype(bf16)
        share_ref[2 * g] = pair[:, :BLOCK]
        share_ref[2 * g + 1] = pair[:, BLOCK:]
        return carry

    lax.fori_loop(0, groups, back, 0)


def shards(tokens, gate_weight, up_weight, gate_keep, up_keep, cotangent):
    rows, cols = lax.axis_size("row"), lax.axis_size("col")
    count, width = tokens.shape
    units = cotangent.shape[1]

    copies = jnp.broadcast_to(tokens[None], (rows, count, width))
    blocks = lax.all_to_all(copies, "row", 0, 0, tiled=True)

    gate_first = (jnp.repeat(gate_keep[0], BLOCK) > 0)[None, :]
    up_first = (jnp.repeat(up_keep[0], BLOCK) > 0)[None, :]
    gate_tile, up_tile = kept(gate_weight, gate_first), kept(up_weight, up_first)
    power = exponent(jnp.maximum(jnp.max(jnp.abs(gate_tile)), jnp.max(jnp.abs(up_tile))))
    scale = jnp.exp2(power)
    line = lax.broadcasted_iota(jnp.int32, (EXTRA, units), 0)
    marks = jnp.where(
        line == 0,
        gate_first.astype(f32),
        jnp.where(line == 1, up_first.astype(f32), jnp.where(line == 2, power, 0.0)),
    )
    packed = jnp.concatenate([gate_tile * scale, up_tile * scale, marks], axis=0).astype(f16)
    weights = lax.all_gather(packed, "col", axis=0)
    back = jnp.exp2(-weights[:, 2 * BLOCK + 2, :1].astype(f32))[:, :, None]
    is_mark = lax.broadcasted_iota(jnp.int32, (1, 2 * BLOCK + EXTRA, 1), 1) >= 2 * BLOCK
    weights = (weights.astype(f32) * jnp.where(is_mark, 1.0, back)).astype(bf16)

    hidden, both, share = pl.pallas_call(
        forward,
        out_shape=(
            jax.ShapeDtypeStruct((count, units), bf16),
            jax.ShapeDtypeStruct((count, 2 * units), bf16),
            jax.ShapeDtypeStruct((rows, count, width), bf16),
        ),
        in_specs=[pl.BlockSpec(memory_space=pltpu.VMEM)] * 3,
        out_specs=[pl.BlockSpec(memory_space=pltpu.VMEM)] * 3,
        scratch_shapes=[
            pltpu.VMEM((count, rows * width), bf16),
            pltpu.VMEM((rows * width, 2 * units), bf16),
        ],
        compiler_params=pltpu.CompilerParams(vmem_limit_bytes=40 * 2**20),
        cost_estimate=pl.CostEstimate(
            flops=8 * count * rows * width * units, bytes_accessed=8 * 2**20, transcendentals=count * units
        ),
    )(blocks, weights, cotangent)

    by_col = blocks.reshape(cols, rows // cols, count, width)
    columns = lax.all_to_all(by_col, "col", 0, 0, tiled=True)

    shares = lax.all_to_all(share, "row", 0, 0, tiled=True)

    both = both.astype(f32)
    power = exponent(jnp.max(jnp.abs(both)))
    sent = jnp.concatenate([both * jnp.exp2(power), jnp.full((8, 2 * units), power)], axis=0)
    both_all = lax.all_gather(sent.astype(f16), "col", axis=0)
    back = jnp.exp2(-both_all[:, count, :1].astype(f32))[:, :, None]
    both_all = (both_all[:, :count].astype(f32) * back).astype(bf16)

    total = jnp.sum(shares.astype(f32), axis=0).astype(bf16)
    row = lax.axis_index("row")
    half = count // 2
    odd = row % 2
    pieces = []
    for flip in range(2):
        route = []
        for r in range(rows):
            for c in range(cols):
                to = (2 * c + ((r % 2) ^ flip)) * cols + r // 2
                route.append((r * cols + c, to))
        piece = jnp.where((odd ^ flip) == 1, total[half:], total[:half])
        pieces.append(lax.ppermute(piece, ("row", "col"), route))
    left = jnp.where(odd == 0, pieces[0], pieces[1])
    right = jnp.where(odd == 0, pieces[1], pieces[0])
    grad_tokens = jnp.concatenate([left, right], axis=1)

    columns = columns.transpose(0, 2, 1, 3).reshape(cols * count, (rows // cols) * width)
    both_all = both_all.reshape(cols * count, 2 * units)
    contract_first = (((0,), (0,)), ((), ()))
    masks = [jnp.repeat(jnp.repeat(k, BLOCK, 0), BLOCK, 1).astype(f32) for k in (gate_keep, up_keep)]
    grads = [
        lax.dot_general(
            columns, both_all[:, i * units : (i + 1) * units], contract_first, preferred_element_type=f32
        ) * masks[i]
        for i in range(2)
    ]
    return hidden, grad_tokens, grads[0], grads[1]


def solution(mesh):
    return jax.shard_map(
        shards,
        mesh=mesh,
        in_specs=(P("col", "row"),) * 6,
        out_specs=(P("col", "row"), P("row", "col"), P("col", "row"), P("col", "row")),
        check_vma=False,
    )
```

```python
import functools

import jax
import jax.numpy as jnp
from jax import lax
from jax.experimental import pallas as pl
from jax.experimental.pallas import tpu as pltpu
from jax.sharding import PartitionSpec as P

BLOCK = 128
EXTRA = 16
SPLIT = 64
bf16 = jnp.bfloat16
f16 = jnp.float16
f32 = jnp.float32


def exponent(largest):
    return jnp.floor(14.0 - jnp.log2(jnp.maximum(largest, 2.0**-100)))


def peak(values):
    return jnp.max(jnp.max(jnp.abs(values), axis=0, keepdims=True), axis=1, keepdims=True)


def pack(gate_ref, up_ref, gate_keep, up_keep, packed_ref):
    units = gate_ref.shape[1]
    line = lax.broadcasted_iota(jnp.int32, (EXTRA, BLOCK), 0)
    tiles, marks = [], []
    for ref, keep in ((gate_ref, gate_keep), (up_ref, up_keep)):
        for j in range(units // BLOCK):
            at = slice(j * BLOCK, (j + 1) * BLOCK)
            first = keep[0, j]
            tiles.append(jnp.where(first > 0, ref[:BLOCK, at], ref[BLOCK:, at]).astype(f32))
            marks.append(first.astype(f32))
    largest = functools.reduce(jnp.maximum, [peak(tile) for tile in tiles])
    power = exponent(largest)
    scale = jnp.exp2(power)
    count = units // BLOCK
    for j in range(count):
        at = slice(j * BLOCK, (j + 1) * BLOCK)
        packed_ref[:BLOCK, at] = (tiles[j] * scale).astype(bf16)
        packed_ref[BLOCK : 2 * BLOCK, at] = (tiles[count + j] * scale).astype(bf16)
        lines = jnp.where(line == 0, marks[j], jnp.where(line == 1, marks[count + j], 0.0))
        packed_ref[2 * BLOCK :, at] = jnp.where(line == 2, power, lines).astype(bf16)


def forward(got_ref, w_ref, grad_ref, block_ref, hidden_ref, sent_ref, share_ref, rows, full, both):
    groups, units = w_ref.shape[0], w_ref.shape[2]
    count = grad_ref.shape[0]

    def expand(g, carry):
        at = pl.ds(pl.multiple_of(g * 2 * BLOCK, BLOCK), BLOCK)
        after = pl.ds(pl.multiple_of(g * 2 * BLOCK + BLOCK, BLOCK), BLOCK)
        marks = w_ref[g, 2 * BLOCK : 2 * BLOCK + EXTRA, :]
        back = jnp.exp2(-marks[2:3, :BLOCK].astype(f32)).astype(bf16)
        rows[:, at] = got_ref[2 * g, :count, :] * back
        rows[:, after] = got_ref[2 * g + 1, :count, :] * back
        for part in range(2):
            columns = pl.ds(part * units, units)
            tile = w_ref[g, part * BLOCK : (part + 1) * BLOCK, :]
            first = marks[part : part + 1]
            full[at, columns] = tile * first
            full[after, columns] = tile * (1 - first)
        return carry

    lax.fori_loop(0, groups, expand, 0)
    step = 256
    largest = jnp.zeros((1, 1), f32)
    for n in range(0, units, step):
        gate = jnp.dot(rows[...], full[:, n : n + step], preferred_element_type=f32)
        up = jnp.dot(rows[...], full[:, units + n : units + n + step], preferred_element_type=f32)
        sigmoid_gate = jax.nn.sigmoid(gate)
        activated = gate * sigmoid_gate
        hidden_ref[:, n : n + step] = (activated * up).astype(bf16)
        grad_out = grad_ref[:, n : n + step].astype(f32)
        d_gate = grad_out * up * sigmoid_gate * (1.0 + gate * (1.0 - sigmoid_gate))
        d_up = grad_out * activated
        largest = jnp.maximum(largest, jnp.maximum(peak(d_gate), peak(d_up)))
        both[:, n : n + step] = d_gate.astype(bf16)
        both[:, units + n : units + n + step] = d_up.astype(bf16)

    power = exponent(largest)
    sent_ref[:count, :] = (both[...].astype(f32) * jnp.exp2(power)).astype(bf16)
    sent_ref[count:, :] = jnp.broadcast_to(power, (EXTRA, 2 * units)).astype(bf16)

    def backward(g, carry):
        at = pl.ds(pl.multiple_of(g * 2 * BLOCK, BLOCK), 2 * BLOCK)
        back = jnp.exp2(-w_ref[g, 2 * BLOCK + 2 : 2 * BLOCK + 3, : 2 * BLOCK].astype(f32))
        pair = lax.dot_general(
            both[...], full[at, :], (((1,), (1,)), ((), ())), preferred_element_type=f32
        )
        pair = (pair * back).astype(bf16)
        share_ref[2 * g, :count, :] = pair[:, :BLOCK]
        share_ref[2 * g + 1, :count, :] = pair[:, BLOCK:]
        share_ref[2 * g, count:, :] = block_ref[SPLIT:, :]
        share_ref[2 * g + 1, count:, :] = block_ref[SPLIT:, :]
        return carry

    lax.fori_loop(0, groups, backward, 0)


def weight_gradients(both_ref, got_ref, shares_ref, gate_keep, up_keep, gate_ref, up_ref, columns):
    sources, count, units = both_ref.shape[0], both_ref.shape[1] - EXTRA, gate_ref.shape[1]
    for c in range(sources):
        back = jnp.exp2(-both_ref[c, count : count + 1, :BLOCK].astype(f32)).astype(bf16)
        for h in range(2):
            tile = jnp.concatenate(
                [got_ref[2 * c + h, count:, :], shares_ref[2 * c + h, count:, :]], axis=0
            )
            columns[h * BLOCK : (h + 1) * BLOCK, c * count : (c + 1) * count] = (tile * back).T
    step = 256
    for ref, keep, start in ((gate_ref, gate_keep, 0), (up_ref, up_keep, units)):
        for n in range(0, units, step):
            at = slice(start + n, start + n + step)
            right = jnp.concatenate([both_ref[c, :count, at] for c in range(sources)], axis=0)
            grad = jnp.dot(columns[...], right, preferred_element_type=f32)
            for h in range(2):
                for j in range(step // BLOCK):
                    tile = grad[h * BLOCK : (h + 1) * BLOCK, j * BLOCK : (j + 1) * BLOCK]
                    mask = keep[h, n // BLOCK + j].astype(f32)
                    ref[h * BLOCK : (h + 1) * BLOCK, n + j * BLOCK : n + (j + 1) * BLOCK] = tile * mask


def kernel(body, outs, specs, scratch, megabytes, flops):
    vmem = pl.BlockSpec(memory_space=pltpu.VMEM)
    smem = pl.BlockSpec(memory_space=pltpu.SMEM)
    return pl.pallas_call(
        body,
        out_shape=[jax.ShapeDtypeStruct(shape, dtype) for shape, dtype in outs],
        in_specs=[smem if s == "s" else vmem for s in specs],
        out_specs=[vmem] * len(outs),
        scratch_shapes=[pltpu.VMEM(shape, bf16) for shape in scratch],
        compiler_params=pltpu.CompilerParams(vmem_limit_bytes=megabytes * 2**20),
        cost_estimate=pl.CostEstimate(flops=flops, bytes_accessed=4 * 2**20, transcendentals=0),
    )


def shards(tokens, gate_weight, up_weight, gate_keep, up_keep, cotangent):
    rows, cols = lax.axis_size("row"), lax.axis_size("col")
    count, width = tokens.shape
    units = cotangent.shape[1]
    row = lax.axis_index("row")
    half = count // 2
    odd = row % 2

    route = [
        (r * cols + c, (2 * c + r % 2) * cols + r // 2) for r in range(rows) for c in range(cols)
    ]
    block = lax.ppermute(tokens, ("row", "col"), route)

    (packed,) = kernel(
        pack, [((2 * BLOCK + EXTRA, units), bf16)], "vvss", [], 8, 4 * BLOCK * units
    )(gate_weight, up_weight, gate_keep, up_keep)
    packed = packed.astype(f16)

    copies = jnp.concatenate([tokens, block[:SPLIT]], axis=0)
    copies = jnp.broadcast_to(copies[None], (rows, count + SPLIT, width))
    copies, packed = lax.optimization_barrier((copies, packed))
    got = lax.all_to_all(copies, "row", 0, 0, tiled=True)

    weights = lax.all_gather(packed, "col", axis=0).astype(bf16)

    hidden, sent, share = kernel(
        forward,
        [
            ((count, units), bf16),
            ((count + EXTRA, 2 * units), bf16),
            ((rows, 2 * count - SPLIT, width), bf16),
        ],
        "vvvv",
        [(count, rows * width), (rows * width, 2 * units), (count, 2 * units)],
        28,
        8 * count * rows * width * units,
    )(got, weights, cotangent, block)

    shares = lax.all_to_all(share, "row", 0, 0, tiled=True)

    both_all = lax.all_gather(sent.astype(f16), "col", axis=0).astype(bf16)

    total = jnp.sum(shares[:, :count].astype(f32), axis=0).astype(bf16)
    pieces = []
    for flip in range(2):
        route = []
        for r in range(rows):
            for c in range(cols):
                to = (2 * c + ((r % 2) ^ flip)) * cols + r // 2
                route.append((r * cols + c, to))
        piece = jnp.where((odd ^ flip) == 1, total[half:], total[:half])
        pieces.append(lax.ppermute(piece, ("row", "col"), route))
    left = jnp.where(odd == 0, pieces[0], pieces[1])
    right = jnp.where(odd == 0, pieces[1], pieces[0])
    grad_tokens = jnp.concatenate([left, right], axis=1)

    grad_gate, grad_up = kernel(
        weight_gradients,
        [((2 * BLOCK, units), f32)] * 2,
        "vvvss",
        [(2 * BLOCK, cols * count)],
        28,
        8 * BLOCK * cols * count * units,
    )(both_all, got, shares, gate_keep, up_keep)
    return hidden, grad_tokens, grad_gate, grad_up


def solution(mesh):
    return jax.shard_map(
        shards,
        mesh=mesh,
        in_specs=(P("col", "row"),) * 6,
        out_specs=(P("col", "row"), P("row", "col"), P("col", "row"), P("col", "row")),
        check_vma=False,
    )
```

```python
import functools

import jax
import jax.numpy as jnp
from jax import lax
from jax.experimental import pallas as pl
from jax.experimental.pallas import tpu as pltpu
from jax.sharding import PartitionSpec as P

BLOCK = 128
EXTRA = 16
MARKS = 8
SPLIT = 64
bf16 = jnp.bfloat16
f16 = jnp.float16
f32 = jnp.float32


def exponent(largest):
    return jnp.floor(14.0 - jnp.log2(jnp.maximum(largest, 2.0**-100)))


def peak(values):
    return jnp.max(jnp.max(jnp.abs(values), axis=0, keepdims=True), axis=1, keepdims=True)


def pack(gate_ref, up_ref, gate_keep, up_keep, packed_ref):
    units = gate_ref.shape[1]
    line = lax.broadcasted_iota(jnp.int32, (EXTRA, BLOCK), 0)
    tiles, marks = [], []
    for ref, keep in ((gate_ref, gate_keep), (up_ref, up_keep)):
        for j in range(units // BLOCK):
            at = slice(j * BLOCK, (j + 1) * BLOCK)
            first = keep[0, j]
            tiles.append(jnp.where(first > 0, ref[:BLOCK, at], ref[BLOCK:, at]).astype(f32))
            marks.append(first.astype(f32))
    largest = functools.reduce(jnp.maximum, [peak(tile) for tile in tiles])
    power = exponent(largest)
    scale = jnp.exp2(power)
    count = units // BLOCK
    for j in range(count):
        at = slice(j * BLOCK, (j + 1) * BLOCK)
        packed_ref[:BLOCK, at] = (tiles[j] * scale).astype(bf16)
        packed_ref[BLOCK : 2 * BLOCK, at] = (tiles[count + j] * scale).astype(bf16)
        lines = jnp.where(line == 0, marks[j], jnp.where(line == 1, marks[count + j], 0.0))
        packed_ref[2 * BLOCK :, at] = jnp.where(line == 2, power, lines).astype(bf16)


def forward(
    got_ref, weights_ref, grad_ref, block_ref, hidden_ref, sent_ref, shares_ref,
    rows, full, both, w_ref, share_ref, in_sems, out_sems,
):
    groups, units = weights_ref.shape[0], weights_ref.shape[2]
    count = grad_ref.shape[0]

    def fetch(g):
        return pltpu.make_async_copy(weights_ref.at[g], w_ref.at[g], in_sems.at[g])

    def deliver(g):
        at = pl.ds(2 * g, 2)
        return pltpu.make_async_copy(share_ref.at[at], shares_ref.at[at], out_sems.at[g])

    def begin(g, carry):
        fetch(g).start()
        return carry

    def expand(g, carry):
        at = pl.ds(pl.multiple_of(g * 2 * BLOCK, BLOCK), BLOCK)
        after = pl.ds(pl.multiple_of(g * 2 * BLOCK + BLOCK, BLOCK), BLOCK)
        fetch(g).wait()
        marks = w_ref[g, 2 * BLOCK :, :]
        back = jnp.exp2(-marks[2:3, :BLOCK].astype(f32)).astype(bf16)
        rows[:, at] = got_ref[2 * g, :count, :] * back
        rows[:, after] = got_ref[2 * g + 1, :count, :] * back
        for part in range(2):
            columns = pl.ds(part * units, units)
            tile = w_ref[g, part * BLOCK : (part + 1) * BLOCK, :]
            first = marks[part : part + 1]
            full[at, columns] = tile * first
            full[after, columns] = tile * (1 - first)
        return carry

    lax.fori_loop(0, groups, begin, 0)
    lax.fori_loop(0, groups, expand, 0)
    step = 256
    largest = jnp.zeros((1, 1), f32)
    for n in range(0, units, step):
        gate = jnp.dot(rows[...], full[:, n : n + step], preferred_element_type=f32)
        up = jnp.dot(rows[...], full[:, units + n : units + n + step], preferred_element_type=f32)
        sigmoid_gate = jax.nn.sigmoid(gate)
        activated = gate * sigmoid_gate
        hidden_ref[:, n : n + step] = (activated * up).astype(bf16)
        grad_out = grad_ref[:, n : n + step].astype(f32)
        d_gate = grad_out * up * sigmoid_gate * (1.0 + gate * (1.0 - sigmoid_gate))
        d_up = grad_out * activated
        largest = jnp.maximum(largest, jnp.maximum(peak(d_gate), peak(d_up)))
        both[:, n : n + step] = d_gate.astype(bf16)
        both[:, units + n : units + n + step] = d_up.astype(bf16)

    power = exponent(largest)
    sent_ref[:count, :] = (both[...].astype(f32) * jnp.exp2(power)).astype(bf16)
    sent_ref[count:, :] = jnp.broadcast_to(power, (EXTRA, 2 * units)).astype(bf16)

    def backward(g, carry):
        at = pl.ds(pl.multiple_of(g * 2 * BLOCK, BLOCK), 2 * BLOCK)
        back = jnp.exp2(-w_ref[g, 2 * BLOCK + 2 : 2 * BLOCK + 3, : 2 * BLOCK].astype(f32))
        pair = lax.dot_general(
            both[...], full[at, :], (((1,), (1,)), ((), ())), preferred_element_type=f32
        )
        pair = (pair * back).astype(bf16)
        share_ref[2 * g, :count, :] = pair[:, :BLOCK]
        share_ref[2 * g + 1, :count, :] = pair[:, BLOCK:]
        share_ref[2 * g, count:, :] = block_ref[SPLIT:, :]
        share_ref[2 * g + 1, count:, :] = block_ref[SPLIT:, :]
        deliver(g).start()
        return carry

    def finish(g, carry):
        deliver(g).wait()
        return carry

    lax.fori_loop(0, groups, backward, 0)
    lax.fori_loop(0, groups, finish, 0)


def weight_gradients(
    both_ref, got_ref, shares_ref, gate_keep, up_keep, gate_ref, up_ref, columns, both, sems
):
    sources, units = both_ref.shape[0], gate_ref.shape[1]
    count = columns.shape[1] // sources

    def fetch(c):
        return pltpu.make_async_copy(both_ref.at[c], both.at[c], sems.at[c])

    for c in range(sources):
        fetch(c).start()
    for c in range(sources):
        fetch(c).wait()
        back = jnp.exp2(-both[c, count : count + 1, :BLOCK].astype(f32)).astype(bf16)
        for h in range(2):
            tile = jnp.concatenate(
                [got_ref[2 * c + h, count:, :], shares_ref[2 * c + h, count:, :]], axis=0
            )
            columns[h * BLOCK : (h + 1) * BLOCK, c * count : (c + 1) * count] = (tile * back).T
    step = 256
    for ref, keep, start in ((gate_ref, gate_keep, 0), (up_ref, up_keep, units)):
        for n in range(0, units, step):
            at = slice(start + n, start + n + step)
            right = jnp.concatenate([both[c, :count, at] for c in range(sources)], axis=0)
            grad = jnp.dot(columns[...], right, preferred_element_type=f32)
            for h in range(2):
                for j in range(step // BLOCK):
                    tile = grad[h * BLOCK : (h + 1) * BLOCK, j * BLOCK : (j + 1) * BLOCK]
                    mask = keep[h, n // BLOCK + j].astype(f32)
                    ref[h * BLOCK : (h + 1) * BLOCK, n + j * BLOCK : n + (j + 1) * BLOCK] = tile * mask


def kernel(body, outs, specs, scratch, sems, megabytes, flops):
    spaces = {"v": pltpu.VMEM, "s": pltpu.SMEM, "h": pltpu.HBM}
    places = [pl.BlockSpec(memory_space=spaces[s]) for s in specs]
    return pl.pallas_call(
        body,
        out_shape=[jax.ShapeDtypeStruct(shape, dtype) for shape, dtype in outs],
        in_specs=places[: -len(outs)],
        out_specs=places[-len(outs) :],
        scratch_shapes=[pltpu.VMEM(shape, bf16) for shape in scratch]
        + [pltpu.SemaphoreType.DMA((n,)) for n in sems],
        compiler_params=pltpu.CompilerParams(vmem_limit_bytes=megabytes * 2**20),
        cost_estimate=pl.CostEstimate(flops=flops, bytes_accessed=4 * 2**20, transcendentals=0),
    )


def shards(tokens, gate_weight, up_weight, gate_keep, up_keep, cotangent):
    rows, cols = lax.axis_size("row"), lax.axis_size("col")
    count, width = tokens.shape
    units = cotangent.shape[1]
    row = lax.axis_index("row")
    half = count // 2
    odd = row % 2

    route = [
        (r * cols + c, (2 * c + r % 2) * cols + r // 2) for r in range(rows) for c in range(cols)
    ]
    block = lax.ppermute(tokens, ("row", "col"), route)

    (packed,) = kernel(
        pack, [((2 * BLOCK + EXTRA, units), bf16)], "vvssv", [], [], 8, 4 * BLOCK * units
    )(gate_weight, up_weight, gate_keep, up_keep)
    packed = packed[: 2 * BLOCK + MARKS].astype(f16)

    copies = jnp.concatenate([tokens, block[:SPLIT]], axis=0)
    copies = jnp.broadcast_to(copies[None], (rows, count + SPLIT, width))
    copies, packed = lax.optimization_barrier((copies, packed))
    got = lax.all_to_all(copies, "row", 0, 0, tiled=True)

    weights = lax.all_gather(packed, "col", axis=0).astype(bf16)

    hidden, sent, share = kernel(
        forward,
        [
            ((count, units), bf16),
            ((count + EXTRA, 2 * units), bf16),
            ((rows, 2 * count - SPLIT, width), bf16),
        ],
        "vhvvvvh",
        [
            (count, rows * width),
            (rows * width, 2 * units),
            (count, 2 * units),
            (cols, 2 * BLOCK + MARKS, units),
            (rows, 2 * count - SPLIT, width),
        ],
        [cols, cols],
        48,
        8 * count * rows * width * units,
    )(got, weights, cotangent, block)

    shares = lax.all_to_all(share, "row", 0, 0, tiled=True)

    both_all = lax.all_gather(sent[: count + MARKS].astype(f16), "col", axis=0).astype(bf16)

    total = jnp.sum(shares[:, :count].astype(f32), axis=0).astype(bf16)
    pieces = []
    for flip in range(2):
        route = []
        for r in range(rows):
            for c in range(cols):
                to = (2 * c + ((r % 2) ^ flip)) * cols + r // 2
                route.append((r * cols + c, to))
        piece = jnp.where((odd ^ flip) == 1, total[half:], total[:half])
        pieces.append(lax.ppermute(piece, ("row", "col"), route))
    left = jnp.where(odd == 0, pieces[0], pieces[1])
    right = jnp.where(odd == 0, pieces[1], pieces[0])
    grad_tokens = jnp.concatenate([left, right], axis=1)

    grad_gate, grad_up = kernel(
        weight_gradients,
        [((2 * BLOCK, units), f32)] * 2,
        "hvvssvv",
        [(2 * BLOCK, cols * count), (cols, count + MARKS, 2 * units)],
        [cols],
        48,
        8 * BLOCK * cols * count * units,
    )(both_all, got, shares, gate_keep, up_keep)
    return hidden, grad_tokens, grad_gate, grad_up


def solution(mesh):
    return jax.shard_map(
        shards,
        mesh=mesh,
        in_specs=(P("col", "row"),) * 6,
        out_specs=(P("col", "row"), P("row", "col"), P("col", "row"), P("col", "row")),
        check_vma=False,
    )
```

```python
import functools

import jax
import jax.numpy as jnp
from jax import lax
from jax.experimental import pallas as pl
from jax.experimental.pallas import tpu as pltpu
from jax.sharding import PartitionSpec as P

BLOCK = 128
EXTRA = 16
MARKS = 8
PARTS = 4
SPLIT = 64
bf16 = jnp.bfloat16
f16 = jnp.float16
f32 = jnp.float32


def exponent(largest):
    return jnp.floor(14.0 - jnp.log2(jnp.maximum(largest, 2.0**-100)))


def peak(values):
    return jnp.max(jnp.max(jnp.abs(values), axis=0, keepdims=True), axis=1, keepdims=True)


def pack(gate_ref, up_ref, gate_keep, up_keep, packed_ref):
    units = gate_ref.shape[1]
    line = lax.broadcasted_iota(jnp.int32, (EXTRA, BLOCK), 0)
    tiles, marks = [], []
    for ref, keep in ((gate_ref, gate_keep), (up_ref, up_keep)):
        for j in range(units // BLOCK):
            at = slice(j * BLOCK, (j + 1) * BLOCK)
            first = keep[0, j]
            tiles.append(jnp.where(first > 0, ref[:BLOCK, at], ref[BLOCK:, at]).astype(f32))
            marks.append(first.astype(f32))
    largest = functools.reduce(jnp.maximum, [peak(tile) for tile in tiles])
    power = exponent(largest)
    scale = jnp.exp2(power)
    count = units // BLOCK
    for j in range(count):
        at = slice(j * BLOCK, (j + 1) * BLOCK)
        packed_ref[:BLOCK, at] = (tiles[j] * scale).astype(bf16)
        packed_ref[BLOCK : 2 * BLOCK, at] = (tiles[count + j] * scale).astype(bf16)
        lines = jnp.where(line == 0, marks[j], jnp.where(line == 1, marks[count + j], 0.0))
        packed_ref[2 * BLOCK :, at] = jnp.where(line == 2, power, lines).astype(bf16)


def spread(tokens_ref, block_ref, copies_ref, one, sems):
    count = tokens_ref.shape[0]
    one[:count] = tokens_ref[...]
    one[count:] = block_ref[:SPLIT]
    copies = [
        pltpu.make_async_copy(one, copies_ref.at[i], sems.at[i]) for i in range(copies_ref.shape[0])
    ]
    for copy in copies:
        copy.start()
    for copy in copies:
        copy.wait()


def forward(
    got_ref, weights_ref, grad_ref, block_ref, hidden_ref, sent_ref, shares_ref,
    rows, full, both, w_ref, share_ref, total, in_sems, out_sems,
):
    groups, units = weights_ref.shape[0], weights_ref.shape[2]
    count = grad_ref.shape[0]
    half, rest = count // 2, (count - SPLIT) // 2

    def fetch(g):
        return pltpu.make_async_copy(weights_ref.at[g], w_ref.at[g], in_sems.at[g])

    def deliver(g):
        at = pl.ds(2 * g, 2)
        return pltpu.make_async_copy(share_ref.at[at], shares_ref.at[at], out_sems.at[g])

    def begin(g, carry):
        fetch(g).start()
        return carry

    def expand(g, carry):
        at = pl.ds(pl.multiple_of(g * 2 * BLOCK, BLOCK), BLOCK)
        after = pl.ds(pl.multiple_of(g * 2 * BLOCK + BLOCK, BLOCK), BLOCK)
        fetch(g).wait()
        marks = w_ref[g, 2 * BLOCK :, :]
        back = jnp.exp2(-marks[2:3, :BLOCK].astype(f32)).astype(bf16)
        rows[:, at] = got_ref[2 * g, :count, :] * back
        rows[:, after] = got_ref[2 * g + 1, :count, :] * back
        for part in range(2):
            columns = pl.ds(part * units, units)
            tile = w_ref[g, part * BLOCK : (part + 1) * BLOCK, :]
            first = marks[part : part + 1]
            full[at, columns] = tile * first
            full[after, columns] = tile * (1 - first)
        return carry

    lax.fori_loop(0, groups, begin, 0)
    part, step = groups // PARTS, 256
    for p in range(PARTS):
        lax.fori_loop(p * part, (p + 1) * part, expand, 0)
        inner = slice(p * part * 2 * BLOCK, (p + 1) * part * 2 * BLOCK)
        for n in range(0, 2 * units, step):
            at = slice(n, n + step)
            term = jnp.dot(rows[:, inner], full[inner, at], preferred_element_type=f32)
            total[:, at] = term if p == 0 else total[:, at] + term

    largest = jnp.zeros((1, 1), f32)
    for n in range(0, units, step):
        gate, up = total[:, n : n + step], total[:, units + n : units + n + step]
        sigmoid_gate = jax.nn.sigmoid(gate)
        activated = gate * sigmoid_gate
        hidden_ref[:, n : n + step] = (activated * up).astype(bf16)
        grad_out = grad_ref[:, n : n + step].astype(f32)
        d_gate = grad_out * up * sigmoid_gate * (1.0 + gate * (1.0 - sigmoid_gate))
        d_up = grad_out * activated
        largest = jnp.maximum(largest, jnp.maximum(peak(d_gate), peak(d_up)))
        both[:, n : n + step] = d_gate.astype(bf16)
        both[:, units + n : units + n + step] = d_up.astype(bf16)

    power = exponent(largest)
    sent_ref[:count, :] = (both[...].astype(f32) * jnp.exp2(power)).astype(bf16)
    sent_ref[count:, :] = jnp.broadcast_to(power, (EXTRA, 2 * units)).astype(bf16)

    def backward(g, carry):
        at = pl.ds(pl.multiple_of(g * 2 * BLOCK, BLOCK), 2 * BLOCK)
        back = jnp.exp2(-w_ref[g, 2 * BLOCK + 2 : 2 * BLOCK + 3, : 2 * BLOCK].astype(f32))
        pair = lax.dot_general(
            both[...], full[at, :], (((1,), (1,)), ((), ())), preferred_element_type=f32
        )
        pair = (pair * back).astype(bf16)
        for i in range(2):
            share_ref[2 * g + i, :half, :] = pair[i * half : (i + 1) * half]
            share_ref[2 * g + i, half:, :BLOCK] = block_ref[SPLIT : SPLIT + rest, :]
            share_ref[2 * g + i, half:, BLOCK:] = block_ref[SPLIT + rest :, :]
        deliver(g).start()
        return carry

    def finish(g, carry):
        deliver(g).wait()
        return carry

    lax.fori_loop(0, groups, backward, 0)
    lax.fori_loop(0, groups, finish, 0)


def weight_gradients(
    both_ref, got_ref, shares_ref, gate_keep, up_keep, gate_ref, up_ref, columns, both, sems
):
    sources, units = both_ref.shape[0], gate_ref.shape[1]
    count = columns.shape[1] // sources

    def fetch(c):
        return pltpu.make_async_copy(both_ref.at[c], both.at[c], sems.at[c])

    for c in range(sources):
        fetch(c).start()
    for c in range(sources):
        fetch(c).wait()
        back = jnp.exp2(-both[c, count : count + 1, :BLOCK].astype(f32)).astype(bf16)
        for h in range(2):
            tile = jnp.concatenate(
                [
                    got_ref[2 * c + h, count:, :],
                    shares_ref[2 * c + h, count // 2 :, :BLOCK],
                    shares_ref[2 * c + h, count // 2 :, BLOCK:],
                ],
                axis=0,
            )
            columns[h * BLOCK : (h + 1) * BLOCK, c * count : (c + 1) * count] = (tile * back).T
    step = 256
    for ref, keep, start in ((gate_ref, gate_keep, 0), (up_ref, up_keep, units)):
        for n in range(0, units, step):
            at = slice(start + n, start + n + step)
            right = jnp.concatenate([both[c, :count, at] for c in range(sources)], axis=0)
            grad = jnp.dot(columns[...], right, preferred_element_type=f32)
            for h in range(2):
                for j in range(step // BLOCK):
                    tile = grad[h * BLOCK : (h + 1) * BLOCK, j * BLOCK : (j + 1) * BLOCK]
                    mask = keep[h, n // BLOCK + j].astype(f32)
                    ref[h * BLOCK : (h + 1) * BLOCK, n + j * BLOCK : n + (j + 1) * BLOCK] = tile * mask


def kernel(body, outs, specs, scratch, sems, megabytes, flops):
    spaces = {"v": pltpu.VMEM, "s": pltpu.SMEM, "h": pltpu.HBM}
    places = [pl.BlockSpec(memory_space=spaces[s]) for s in specs]
    return pl.pallas_call(
        body,
        out_shape=[jax.ShapeDtypeStruct(shape, dtype) for shape, dtype in outs],
        in_specs=places[: -len(outs)],
        out_specs=places[-len(outs) :],
        scratch_shapes=[
            pltpu.VMEM(shape[1:], f32) if shape[0] is f32 else pltpu.VMEM(shape, bf16)
            for shape in scratch
        ]
        + [pltpu.SemaphoreType.DMA((n,)) for n in sems],
        compiler_params=pltpu.CompilerParams(vmem_limit_bytes=megabytes * 2**20),
        cost_estimate=pl.CostEstimate(flops=flops, bytes_accessed=4 * 2**20, transcendentals=0),
    )


def shards(tokens, gate_weight, up_weight, gate_keep, up_keep, cotangent):
    rows, cols = lax.axis_size("row"), lax.axis_size("col")
    count, width = tokens.shape
    units = cotangent.shape[1]

    route = [
        (r * cols + c, (2 * c + r % 2) * cols + r // 2) for r in range(rows) for c in range(cols)
    ]
    block = lax.ppermute(tokens, ("row", "col"), route)

    (packed,) = kernel(
        pack, [((2 * BLOCK + EXTRA, units), bf16)], "vvssv", [], [], 8, 4 * BLOCK * units
    )(gate_weight, up_weight, gate_keep, up_keep)
    packed = packed[: 2 * BLOCK + MARKS].astype(f16)

    (copies,) = kernel(
        spread, [((rows, count + SPLIT, width), bf16)], "vvh", [(count + SPLIT, width)], [rows], 48, 1
    )(tokens, block)
    copies, packed = lax.optimization_barrier((copies, packed))
    got = lax.all_to_all(copies, "row", 0, 0, tiled=True)

    weights = lax.all_gather(packed, "col", axis=0).astype(bf16)

    hidden, sent, share = kernel(
        forward,
        [
            ((count, units), bf16),
            ((count + EXTRA, 2 * units), bf16),
            ((rows, count - SPLIT // 2, 2 * width), bf16),
        ],
        "vhvvvvh",
        [
            (count, rows * width),
            (rows * width, 2 * units),
            (count, 2 * units),
            (cols, 2 * BLOCK + MARKS, units),
            (rows, count - SPLIT // 2, 2 * width),
            (f32, count, 2 * units),
        ],
        [cols, cols],
        48,
        8 * count * rows * width * units,
    )(got, weights, cotangent, block)

    shares = lax.all_to_all(share, "row", 0, 0, tiled=True)

    both_all = lax.all_gather(sent[: count + MARKS].astype(f16), "col", axis=0).astype(bf16)

    total = jnp.sum(shares[:, : count // 2].astype(f32), axis=0).astype(bf16)
    grad_tokens = lax.ppermute(total, ("row", "col"), route)

    grad_gate, grad_up = kernel(
        weight_gradients,
        [((2 * BLOCK, units), f32)] * 2,
        "hvvssvv",
        [(2 * BLOCK, cols * count), (cols, count + MARKS, 2 * units)],
        [cols],
        48,
        8 * BLOCK * cols * count * units,
    )(both_all, got, shares, gate_keep, up_keep)
    return hidden, grad_tokens, grad_gate, grad_up


def solution(mesh):
    return jax.shard_map(
        shards,
        mesh=mesh,
        in_specs=(P("col", "row"),) * 6,
        out_specs=(P("col", "row"), P("row", "col"), P("col", "row"), P("col", "row")),
        check_vma=False,
    )
```

```python
import functools

import jax
import jax.numpy as jnp
from jax import lax
from jax.experimental import pallas as pl
from jax.experimental.pallas import tpu as pltpu
from jax.sharding import PartitionSpec as P

BLOCK = 128
EXTRA = 16
MARKS = 8
PARTS = 4
SPLIT = 64
bf16 = jnp.bfloat16
f16 = jnp.float16
f32 = jnp.float32


def exponent(largest):
    return jnp.floor(14.0 - jnp.log2(jnp.maximum(largest, 2.0**-100)))


def peak(values):
    return jnp.max(jnp.max(jnp.abs(values), axis=0, keepdims=True), axis=1, keepdims=True)


def pack(gate_ref, up_ref, gate_keep, up_keep, packed_ref):
    units = gate_ref.shape[1]
    line = lax.broadcasted_iota(jnp.int32, (EXTRA, BLOCK), 0)
    tiles, marks = [], []
    for ref, keep in ((gate_ref, gate_keep), (up_ref, up_keep)):
        for j in range(units // BLOCK):
            at = slice(j * BLOCK, (j + 1) * BLOCK)
            first = keep[0, j]
            tiles.append(jnp.where(first > 0, ref[:BLOCK, at], ref[BLOCK:, at]).astype(f32))
            marks.append(first.astype(f32))
    largest = functools.reduce(jnp.maximum, [peak(tile) for tile in tiles])
    power = exponent(largest)
    scale = jnp.exp2(power)
    count = units // BLOCK
    for j in range(count):
        at = slice(j * BLOCK, (j + 1) * BLOCK)
        packed_ref[:BLOCK, at] = (tiles[j] * scale).astype(bf16)
        packed_ref[BLOCK : 2 * BLOCK, at] = (tiles[count + j] * scale).astype(bf16)
        lines = jnp.where(line == 0, marks[j], jnp.where(line == 1, marks[count + j], 0.0))
        packed_ref[2 * BLOCK :, at] = jnp.where(line == 2, power, lines).astype(bf16)


def spread(tokens_ref, block_ref, copies_ref, one, sems):
    count = tokens_ref.shape[0]
    one[:count] = tokens_ref[...]
    one[count:] = block_ref[:SPLIT]
    copies = [
        pltpu.make_async_copy(one, copies_ref.at[i], sems.at[i]) for i in range(copies_ref.shape[0])
    ]
    for copy in copies:
        copy.start()
    for copy in copies:
        copy.wait()


def forward(
    got_ref, weights_ref, grad_ref, block_ref, hidden_ref, sent_ref, share_ref,
    rows, full, both, w_ref, turned, total, sems,
):
    groups, units = weights_ref.shape[0], weights_ref.shape[2]
    count = grad_ref.shape[0]
    half = count // 2

    def fetch(g):
        return pltpu.make_async_copy(weights_ref.at[g], w_ref.at[g], sems.at[g])

    def begin(g, carry):
        fetch(g).start()
        return carry

    def expand(g, carry):
        at = pl.ds(pl.multiple_of(g * 2 * BLOCK, BLOCK), BLOCK)
        after = pl.ds(pl.multiple_of(g * 2 * BLOCK + BLOCK, BLOCK), BLOCK)
        fetch(g).wait()
        marks = w_ref[g, 2 * BLOCK :, :]
        back = jnp.exp2(-marks[2:3, :BLOCK].astype(f32)).astype(bf16)
        rows[:, at] = got_ref[2 * g, :count, :] * back
        rows[:, after] = got_ref[2 * g + 1, :count, :] * back
        for part in range(2):
            columns = pl.ds(part * units, units)
            tile = w_ref[g, part * BLOCK : (part + 1) * BLOCK, :]
            first = marks[part : part + 1]
            full[at, columns] = tile * first
            full[after, columns] = tile * (1 - first)
        return carry

    lax.fori_loop(0, groups, begin, 0)
    part, step = groups // PARTS, 256
    for p in range(PARTS):
        lax.fori_loop(p * part, (p + 1) * part, expand, 0, unroll=part)
        inner = slice(p * part * 2 * BLOCK, (p + 1) * part * 2 * BLOCK)
        for n in range(0, 2 * units, step):
            at = slice(n, n + step)
            term = jnp.dot(rows[:, inner], full[inner, at], preferred_element_type=f32)
            total[:, at] = term if p == 0 else total[:, at] + term

    largest = jnp.zeros((1, 1), f32)
    for n in range(0, units, step):
        gate, up = total[:, n : n + step], total[:, units + n : units + n + step]
        sigmoid_gate = jax.nn.sigmoid(gate)
        activated = gate * sigmoid_gate
        hidden_ref[:, n : n + step] = (activated * up).astype(bf16)
        grad_out = grad_ref[:, n : n + step].astype(f32)
        d_gate = grad_out * up * sigmoid_gate * (1.0 + gate * (1.0 - sigmoid_gate))
        d_up = grad_out * activated
        largest = jnp.maximum(largest, jnp.maximum(peak(d_gate), peak(d_up)))
        both[:, n : n + step] = d_gate.astype(bf16)
        both[:, units + n : units + n + step] = d_up.astype(bf16)

    power = exponent(largest)
    sent_ref[:count, :] = (both[...].astype(f32) * jnp.exp2(power)).astype(bf16)
    sent_ref[count:, :] = jnp.broadcast_to(power, (EXTRA, 2 * units)).astype(bf16)

    turned[...] = both[...].T
    left = lax.broadcasted_iota(jnp.int32, (BLOCK, count), 1) < half

    def backward(g, carry):
        at = pl.ds(pl.multiple_of(g * 2 * BLOCK, BLOCK), 2 * BLOCK)
        back = jnp.exp2(-w_ref[g, 2 * BLOCK + 2 : 2 * BLOCK + 3, :count].astype(f32))
        pair = jnp.dot(full[at, :], turned[...], preferred_element_type=f32) * back
        upper, lower = pair[:BLOCK], pair[BLOCK:]
        first = jnp.where(left, upper, pltpu.roll(lower, half, 1))
        second = jnp.where(left, pltpu.roll(upper, half, 1), lower)
        share_ref[2 * g, :BLOCK, :] = first.astype(bf16)
        share_ref[2 * g + 1, :BLOCK, :] = second.astype(bf16)
        share_ref[2 * g, BLOCK:, :] = block_ref[SPLIT:, :]
        share_ref[2 * g + 1, BLOCK:, :] = block_ref[SPLIT:, :]
        return carry

    lax.fori_loop(0, groups, backward, 0, unroll=groups)


def add_up(shares_ref, out_ref):
    half = out_ref.shape[0]
    total = shares_ref[0, :BLOCK, :].astype(f32)
    for i in range(1, shares_ref.shape[0]):
        total = total + shares_ref[i, :BLOCK, :].astype(f32)
    total = total.T
    out_ref[:, :BLOCK] = total[:half].astype(bf16)
    out_ref[:, BLOCK:] = total[half:].astype(bf16)


def weight_gradients(
    both_ref, got_ref, shares_ref, gate_keep, up_keep, gate_ref, up_ref, columns, both, total, sems
):
    sources, units = both_ref.shape[0], gate_ref.shape[1]
    count = columns.shape[1] // sources

    def fetch(c):
        return pltpu.make_async_copy(both_ref.at[c], both.at[c], sems.at[c])

    for c in range(sources):
        fetch(c).start()
    part, step = sources // PARTS, 256
    for p in range(PARTS):
        for c in range(p * part, (p + 1) * part):
            fetch(c).wait()
            back = jnp.exp2(-both[c, count : count + 1, :BLOCK].astype(f32)).astype(bf16)
            for h in range(2):
                tile = jnp.concatenate(
                    [got_ref[2 * c + h, count:, :], shares_ref[2 * c + h, BLOCK:, :]], axis=0
                )
                columns[h * BLOCK : (h + 1) * BLOCK, c * count : (c + 1) * count] = (tile * back).T
        inner = slice(p * part * count, (p + 1) * part * count)
        for n in range(0, 2 * units, step):
            at = slice(n, n + step)
            right = jnp.concatenate(
                [both[c, :count, at] for c in range(p * part, (p + 1) * part)], axis=0
            )
            term = jnp.dot(columns[:, inner], right, preferred_element_type=f32)
            if p > 0:
                term = total[:, at] + term
            if p < PARTS - 1:
                total[:, at] = term
                continue
            ref, keep = (gate_ref, gate_keep) if n < units else (up_ref, up_keep)
            for h in range(2):
                for j in range(step // BLOCK):
                    tile = term[h * BLOCK : (h + 1) * BLOCK, j * BLOCK : (j + 1) * BLOCK]
                    start = n % units + j * BLOCK
                    mask = keep[h, start // BLOCK].astype(f32)
                    ref[h * BLOCK : (h + 1) * BLOCK, start : start + BLOCK] = tile * mask


def kernel(body, outs, specs, scratch, sems, megabytes, flops):
    spaces = {"v": pltpu.VMEM, "s": pltpu.SMEM, "h": pltpu.HBM}
    places = [pl.BlockSpec(memory_space=spaces[s]) for s in specs]
    return pl.pallas_call(
        body,
        out_shape=[jax.ShapeDtypeStruct(shape, dtype) for shape, dtype in outs],
        in_specs=places[: -len(outs)],
        out_specs=places[-len(outs) :],
        scratch_shapes=[
            pltpu.VMEM(shape[1:], f32) if shape[0] is f32 else pltpu.VMEM(shape, bf16)
            for shape in scratch
        ]
        + [pltpu.SemaphoreType.DMA((n,)) for n in sems],
        compiler_params=pltpu.CompilerParams(vmem_limit_bytes=megabytes * 2**20),
        cost_estimate=pl.CostEstimate(flops=flops, bytes_accessed=4 * 2**20, transcendentals=0),
    )


def shards(tokens, gate_weight, up_weight, gate_keep, up_keep, cotangent):
    rows, cols = lax.axis_size("row"), lax.axis_size("col")
    count, width = tokens.shape
    units = cotangent.shape[1]

    route = [
        (r * cols + c, (2 * c + r % 2) * cols + r // 2) for r in range(rows) for c in range(cols)
    ]
    block = lax.ppermute(tokens, ("row", "col"), route)

    (packed,) = kernel(
        pack, [((2 * BLOCK + EXTRA, units), bf16)], "vvssv", [], [], 8, 4 * BLOCK * units
    )(gate_weight, up_weight, gate_keep, up_keep)
    packed = packed[: 2 * BLOCK + MARKS].astype(f16)

    (copies,) = kernel(
        spread, [((rows, count + SPLIT, width), bf16)], "vvh", [(count + SPLIT, width)], [rows], 48, 1
    )(tokens, block)
    copies, packed = lax.optimization_barrier((copies, packed))
    got = lax.all_to_all(copies, "row", 0, 0, tiled=True)

    weights = lax.all_gather(packed, "col", axis=0).astype(bf16)

    hidden, sent, share = kernel(
        forward,
        [
            ((count, units), bf16),
            ((count + EXTRA, 2 * units), bf16),
            ((rows, BLOCK + count - SPLIT, count), bf16),
        ],
        "vhvvvvv",
        [
            (count, rows * width),
            (rows * width, 2 * units),
            (count, 2 * units),
            (cols, 2 * BLOCK + MARKS, units),
            (2 * units, count),
            (f32, count, 2 * units),
        ],
        [cols],
        48,
        8 * count * rows * width * units,
    )(got, weights, cotangent, block)

    shares = lax.all_to_all(share, "row", 0, 0, tiled=True)

    both_all = lax.all_gather(sent[: count + MARKS].astype(f16), "col", axis=0).astype(bf16)

    (total,) = kernel(add_up, [((count // 2, 2 * width), bf16)], "vv", [], [], 48, 10**6)(shares)
    grad_tokens = lax.ppermute(total, ("row", "col"), route)

    grad_gate, grad_up = kernel(
        weight_gradients,
        [((2 * BLOCK, units), f32)] * 2,
        "hvvssvv",
        [(2 * BLOCK, cols * count), (cols, count + MARKS, 2 * units), (f32, 2 * BLOCK, 2 * units)],
        [cols],
        48,
        8 * BLOCK * cols * count * units,
    )(both_all, got, shares, gate_keep, up_keep)
    return hidden, grad_tokens, grad_gate, grad_up


def solution(mesh):
    return jax.shard_map(
        shards,
        mesh=mesh,
        in_specs=(P("col", "row"),) * 6,
        out_specs=(P("col", "row"), P("row", "col"), P("col", "row"), P("col", "row")),
        check_vma=False,
    )
```

```python
import functools

import jax
import jax.numpy as jnp
from jax import lax
from jax.experimental import pallas as pl
from jax.experimental.pallas import tpu as pltpu
from jax.sharding import PartitionSpec as P

BLOCK = 128
EXTRA = 16
MARKS = 8
PARTS = 4
SPLIT = 64
bf16 = jnp.bfloat16
f16 = jnp.float16
f32 = jnp.float32


def exponent(largest):
    return jnp.floor(14.0 - jnp.log2(jnp.maximum(largest, 2.0**-100)))


def peak(values):
    return jnp.max(jnp.max(jnp.abs(values), axis=0, keepdims=True), axis=1, keepdims=True)


def pack(gate_ref, up_ref, tokens_ref, gate_keep, up_keep, packed_ref, same_ref):
    units = gate_ref.shape[1]
    same_ref[...] = tokens_ref[...]
    line = lax.broadcasted_iota(jnp.int32, (EXTRA, BLOCK), 0)
    tiles, marks = [], []
    for ref, keep in ((gate_ref, gate_keep), (up_ref, up_keep)):
        for j in range(units // BLOCK):
            at = slice(j * BLOCK, (j + 1) * BLOCK)
            first = keep[0, j]
            tiles.append(jnp.where(first > 0, ref[:BLOCK, at], ref[BLOCK:, at]).astype(f32))
            marks.append(first.astype(f32))
    largest = functools.reduce(jnp.maximum, [peak(tile) for tile in tiles])
    power = exponent(largest)
    scale = jnp.exp2(power)
    count = units // BLOCK
    for j in range(count):
        at = slice(j * BLOCK, (j + 1) * BLOCK)
        packed_ref[:BLOCK, at] = (tiles[j] * scale).astype(bf16)
        packed_ref[BLOCK : 2 * BLOCK, at] = (tiles[count + j] * scale).astype(bf16)
        lines = jnp.where(line == 0, marks[j], jnp.where(line == 1, marks[count + j], 0.0))
        packed_ref[2 * BLOCK :, at] = jnp.where(line == 2, power, lines).astype(bf16)


def spread(tokens_ref, block_ref, copies_ref, one, sems):
    count = tokens_ref.shape[0]
    one[:count] = tokens_ref[...]
    one[count:] = block_ref[:SPLIT]
    copies = [
        pltpu.make_async_copy(one, copies_ref.at[i], sems.at[i]) for i in range(copies_ref.shape[0])
    ]
    for copy in copies:
        copy.start()
    for copy in copies:
        copy.wait()


def forward(
    got_ref, weights_ref, grad_ref, block_ref, hidden_ref, sent_ref, share_ref,
    rows, full, both, w_ref, turned, total, sems,
):
    groups, units = weights_ref.shape[0], weights_ref.shape[2]
    count = grad_ref.shape[0]
    half = count // 2

    def fetch(g):
        return pltpu.make_async_copy(weights_ref.at[g], w_ref.at[g], sems.at[g])

    def begin(g, carry):
        fetch(g).start()
        return carry

    def expand(g, carry):
        at = pl.ds(pl.multiple_of(g * 2 * BLOCK, BLOCK), BLOCK)
        after = pl.ds(pl.multiple_of(g * 2 * BLOCK + BLOCK, BLOCK), BLOCK)
        fetch(g).wait()
        marks = w_ref[g, 2 * BLOCK :, :]
        back = jnp.exp2(-marks[2:3, :BLOCK].astype(f32)).astype(bf16)
        rows[:, at] = got_ref[2 * g, :count, :] * back
        rows[:, after] = got_ref[2 * g + 1, :count, :] * back
        for part in range(2):
            columns = pl.ds(part * units, units)
            tile = w_ref[g, part * BLOCK : (part + 1) * BLOCK, :]
            first = marks[part : part + 1]
            full[at, columns] = tile * first
            full[after, columns] = tile * (1 - first)
        return carry

    lax.fori_loop(0, groups, begin, 0)
    part, step = groups // PARTS, 256
    for p in range(PARTS):
        lax.fori_loop(p * part, (p + 1) * part, expand, 0, unroll=part)
        inner = slice(p * part * 2 * BLOCK, (p + 1) * part * 2 * BLOCK)
        for n in range(0, 2 * units, step):
            at = slice(n, n + step)
            term = jnp.dot(rows[:, inner], full[inner, at], preferred_element_type=f32)
            total[:, at] = term if p == 0 else total[:, at] + term

    largest = jnp.zeros((1, 1), f32)
    for n in range(0, units, step):
        gate, up = total[:, n : n + step], total[:, units + n : units + n + step]
        sigmoid_gate = jax.nn.sigmoid(gate)
        activated = gate * sigmoid_gate
        hidden_ref[:, n : n + step] = (activated * up).astype(bf16)
        grad_out = grad_ref[:, n : n + step].astype(f32)
        d_gate = grad_out * up * sigmoid_gate * (1.0 + gate * (1.0 - sigmoid_gate))
        d_up = grad_out * activated
        largest = jnp.maximum(largest, jnp.maximum(peak(d_gate), peak(d_up)))
        both[:, n : n + step] = d_gate.astype(bf16)
        both[:, units + n : units + n + step] = d_up.astype(bf16)

    power = exponent(largest)
    scaled = (both[...].astype(f32) * jnp.exp2(power)).astype(bf16)
    sent_ref[:count, :] = scaled[:, :units]
    sent_ref[count : 2 * count, :] = scaled[:, units:]
    sent_ref[2 * count :, :] = jnp.broadcast_to(power, (EXTRA, units)).astype(bf16)

    turned[...] = both[...].T
    left = lax.broadcasted_iota(jnp.int32, (BLOCK, count), 1) < half

    def backward(g, carry):
        at = pl.ds(pl.multiple_of(g * 2 * BLOCK, BLOCK), 2 * BLOCK)
        back = jnp.exp2(-w_ref[g, 2 * BLOCK + 2 : 2 * BLOCK + 3, :count].astype(f32))
        pair = jnp.dot(full[at, :], turned[...], preferred_element_type=f32) * back
        upper, lower = pair[:BLOCK], pair[BLOCK:]
        first = jnp.where(left, upper, pltpu.roll(lower, half, 1))
        second = jnp.where(left, pltpu.roll(upper, half, 1), lower)
        share_ref[2 * g, :BLOCK, :] = first.astype(bf16)
        share_ref[2 * g + 1, :BLOCK, :] = second.astype(bf16)
        share_ref[2 * g, BLOCK:, :] = block_ref[SPLIT:, :]
        share_ref[2 * g + 1, BLOCK:, :] = block_ref[SPLIT:, :]
        return carry

    lax.fori_loop(0, groups, backward, 0, unroll=groups)


def add_up(shares_ref, out_ref):
    half = out_ref.shape[0]
    total = shares_ref[0, :BLOCK, :].astype(f32)
    for i in range(1, shares_ref.shape[0]):
        total = total + shares_ref[i, :BLOCK, :].astype(f32)
    total = total.T
    out_ref[:, :BLOCK] = total[:half].astype(bf16)
    out_ref[:, BLOCK:] = total[half:].astype(bf16)


def weight_gradients(
    both_ref, got_ref, shares_ref, gate_keep, up_keep, gate_ref, up_ref, columns, both, total, sems, out_sems
):
    sources, units = both_ref.shape[0], gate_ref.shape[1]
    count = columns.shape[1] // sources

    def fetch(c):
        return pltpu.make_async_copy(both_ref.at[c], both.at[c], sems.at[c])

    for c in range(sources):
        fetch(c).start()
    part, step = sources // PARTS, 256
    copies = []
    for p in range(PARTS):
        for c in range(p * part, (p + 1) * part):
            fetch(c).wait()
            back = jnp.exp2(-both[c, 2 * count : 2 * count + 1, :BLOCK].astype(f32)).astype(bf16)
            for h in range(2):
                tile = jnp.concatenate(
                    [got_ref[2 * c + h, count:, :], shares_ref[2 * c + h, BLOCK:, :]], axis=0
                )
                columns[h * BLOCK : (h + 1) * BLOCK, c * count : (c + 1) * count] = (tile * back).T
        inner = slice(p * part * count, (p + 1) * part * count)
        for n in range(0, 2 * units, step):
            at, start = slice(n, n + step), n % units
            lines = slice(0, count) if n < units else slice(count, 2 * count)
            right = jnp.concatenate(
                [both[c, lines, start : start + step] for c in range(p * part, (p + 1) * part)],
                axis=0,
            )
            term = jnp.dot(columns[:, inner], right, preferred_element_type=f32)
            if p > 0:
                term = total[:, at] + term
            if p < PARTS - 1:
                total[:, at] = term
                continue
            ref, keep = (gate_ref, gate_keep) if n < units else (up_ref, up_keep)
            for h in range(2):
                for j in range(step // BLOCK):
                    tile = term[h * BLOCK : (h + 1) * BLOCK, j * BLOCK : (j + 1) * BLOCK]
                    mask = keep[h, start // BLOCK + j].astype(f32)
                    column = n + j * BLOCK
                    total[h * BLOCK : (h + 1) * BLOCK, column : column + BLOCK] = tile * mask
            copy = pltpu.make_async_copy(
                total.at[:, pl.ds(n, step)], ref.at[:, pl.ds(start, step)], out_sems.at[n // step]
            )
            copy.start()
            copies.append(copy)
    for copy in copies:
        copy.wait()


def kernel(body, outs, specs, scratch, sems, megabytes, flops):
    spaces = {"v": pltpu.VMEM, "s": pltpu.SMEM, "h": pltpu.HBM}
    places = [pl.BlockSpec(memory_space=spaces[s]) for s in specs]
    return pl.pallas_call(
        body,
        out_shape=[jax.ShapeDtypeStruct(shape, dtype) for shape, dtype in outs],
        in_specs=places[: -len(outs)],
        out_specs=places[-len(outs) :],
        scratch_shapes=[
            pltpu.VMEM(shape[1:], f32) if shape[0] is f32 else pltpu.VMEM(shape, bf16)
            for shape in scratch
        ]
        + [pltpu.SemaphoreType.DMA((n,)) for n in sems],
        compiler_params=pltpu.CompilerParams(vmem_limit_bytes=megabytes * 2**20),
        cost_estimate=pl.CostEstimate(flops=flops, bytes_accessed=4 * 2**20, transcendentals=0),
    )


def shards(tokens, gate_weight, up_weight, gate_keep, up_keep, cotangent):
    rows, cols = lax.axis_size("row"), lax.axis_size("col")
    count, width = tokens.shape
    units = cotangent.shape[1]

    route = [
        (r * cols + c, (2 * c + r % 2) * cols + r // 2) for r in range(rows) for c in range(cols)
    ]
    block = lax.ppermute(tokens, ("row", "col"), route)

    packed, same = kernel(
        pack,
        [((2 * BLOCK + EXTRA, units), bf16), ((count, width), bf16)],
        "vvvssvv",
        [],
        [],
        8,
        4 * BLOCK * units,
    )(gate_weight, up_weight, tokens, gate_keep, up_keep)
    packed = packed[: 2 * BLOCK + MARKS].astype(f16)

    (copies,) = kernel(
        spread, [((rows, count + SPLIT, width), bf16)], "vvh", [(count + SPLIT, width)], [rows], 48, 1
    )(same, block)
    copies, packed = lax.optimization_barrier((copies, packed))
    got = lax.all_to_all(copies, "row", 0, 0, tiled=True)

    weights = lax.all_gather(packed, "col", axis=0).astype(bf16)

    hidden, sent, share = kernel(
        forward,
        [
            ((count, units), bf16),
            ((2 * count + EXTRA, units), bf16),
            ((rows, BLOCK + count - SPLIT, count), bf16),
        ],
        "vhvvvvv",
        [
            (count, rows * width),
            (rows * width, 2 * units),
            (count, 2 * units),
            (cols, 2 * BLOCK + MARKS, units),
            (2 * units, count),
            (f32, count, 2 * units),
        ],
        [cols],
        48,
        8 * count * rows * width * units,
    )(got, weights, cotangent, block)

    shares = lax.all_to_all(share, "row", 0, 0, tiled=True)

    both_all = lax.all_gather(sent[: 2 * count + MARKS].astype(f16), "col", axis=0).astype(bf16)

    (total,) = kernel(add_up, [((count // 2, 2 * width), bf16)], "vv", [], [], 48, 10**6)(shares)
    grad_tokens = lax.ppermute(total, ("row", "col"), route)

    grad_gate, grad_up = kernel(
        weight_gradients,
        [((2 * BLOCK, units), f32)] * 2,
        "hvvsshh",
        [(2 * BLOCK, cols * count), (cols, 2 * count + MARKS, units), (f32, 2 * BLOCK, 2 * units)],
        [cols, 4],
        48,
        8 * BLOCK * cols * count * units,
    )(both_all, got, shares, gate_keep, up_keep)
    return hidden, grad_tokens, grad_gate, grad_up


def solution(mesh):
    return jax.shard_map(
        shards,
        mesh=mesh,
        in_specs=(P("col", "row"),) * 6,
        out_specs=(P("col", "row"), P("row", "col"), P("col", "row"), P("col", "row")),
        check_vma=False,
    )
```

```python
import functools

import jax
import jax.numpy as jnp
from jax import lax
from jax.experimental import pallas as pl
from jax.experimental.pallas import tpu as pltpu
from jax.sharding import PartitionSpec as P

BLOCK = 128
EXTRA = 16
MARKS = 8
PARTS = 4
SPLIT = 64
bf16 = jnp.bfloat16
f16 = jnp.float16
f32 = jnp.float32


def exponent(largest):
    return jnp.floor(14.0 - jnp.log2(jnp.maximum(largest, 2.0**-100)))


def peak(values):
    return jnp.max(jnp.max(jnp.abs(values), axis=0, keepdims=True), axis=1, keepdims=True)


def pack(gate_ref, up_ref, tokens_ref, gate_keep, up_keep, packed_ref, same_ref):
    units = gate_ref.shape[1]
    same_ref[...] = tokens_ref[...]
    line = lax.broadcasted_iota(jnp.int32, (EXTRA, BLOCK), 0)
    tiles, marks = [], []
    for ref, keep in ((gate_ref, gate_keep), (up_ref, up_keep)):
        for j in range(units // BLOCK):
            at = slice(j * BLOCK, (j + 1) * BLOCK)
            first = keep[0, j]
            tiles.append(jnp.where(first > 0, ref[:BLOCK, at], ref[BLOCK:, at]).astype(f32))
            marks.append(first.astype(f32))
    largest = functools.reduce(jnp.maximum, [peak(tile) for tile in tiles])
    power = exponent(largest)
    scale = jnp.exp2(power)
    count = units // BLOCK
    for j in range(count):
        at = slice(j * BLOCK, (j + 1) * BLOCK)
        packed_ref[:BLOCK, at] = (tiles[j] * scale).astype(bf16)
        packed_ref[BLOCK : 2 * BLOCK, at] = (tiles[count + j] * scale).astype(bf16)
        lines = jnp.where(line == 0, marks[j], jnp.where(line == 1, marks[count + j], 0.0))
        packed_ref[2 * BLOCK :, at] = jnp.where(line == 2, power, lines).astype(bf16)


def spread(tokens_ref, block_ref, copies_ref, one, sems):
    count = tokens_ref.shape[0]
    one[:count] = tokens_ref[...]
    one[count:] = block_ref[:SPLIT]
    copies = [
        pltpu.make_async_copy(one, copies_ref.at[i], sems.at[i]) for i in range(copies_ref.shape[0])
    ]
    for copy in copies:
        copy.start()
    for copy in copies:
        copy.wait()


def forward(
    got_ref, weights_ref, grad_ref, block_ref, hidden_ref, sent_ref, shares_ref,
    rows, full, both, w_ref, share_ref, turned, total, sems, out_sems,
):
    groups, units = weights_ref.shape[0], weights_ref.shape[2]
    count = grad_ref.shape[0]
    half = count // 2

    def fetch(g):
        return pltpu.make_async_copy(weights_ref.at[g], w_ref.at[g], sems.at[g])

    def deliver(g):
        at = pl.ds(2 * g, 2)
        return pltpu.make_async_copy(share_ref.at[at], shares_ref.at[at], out_sems.at[g])

    def begin(g, carry):
        fetch(g).start()
        return carry

    def expand(g, carry):
        at = pl.ds(pl.multiple_of(g * 2 * BLOCK, BLOCK), BLOCK)
        after = pl.ds(pl.multiple_of(g * 2 * BLOCK + BLOCK, BLOCK), BLOCK)
        fetch(g).wait()
        marks = w_ref[g, 2 * BLOCK :, :]
        back = jnp.exp2(-marks[2:3, :BLOCK].astype(f32)).astype(bf16)
        rows[:, at] = got_ref[2 * g, :count, :] * back
        rows[:, after] = got_ref[2 * g + 1, :count, :] * back
        for part in range(2):
            columns = pl.ds(part * units, units)
            tile = w_ref[g, part * BLOCK : (part + 1) * BLOCK, :]
            first = marks[part : part + 1]
            full[at, columns] = tile * first
            full[after, columns] = tile * (1 - first)
        return carry

    lax.fori_loop(0, groups, begin, 0)
    part, step = groups // PARTS, 256
    for p in range(PARTS):
        lax.fori_loop(p * part, (p + 1) * part, expand, 0, unroll=part)
        inner = slice(p * part * 2 * BLOCK, (p + 1) * part * 2 * BLOCK)
        for n in range(0, 2 * units, step):
            at = slice(n, n + step)
            term = jnp.dot(rows[:, inner], full[inner, at], preferred_element_type=f32)
            total[:, at] = term if p == 0 else total[:, at] + term

    largest = jnp.zeros((1, 1), f32)
    for n in range(0, units, step):
        gate, up = total[:, n : n + step], total[:, units + n : units + n + step]
        sigmoid_gate = jax.nn.sigmoid(gate)
        activated = gate * sigmoid_gate
        hidden_ref[:, n : n + step] = (activated * up).astype(bf16)
        grad_out = grad_ref[:, n : n + step].astype(f32)
        d_gate = grad_out * up * sigmoid_gate * (1.0 + gate * (1.0 - sigmoid_gate))
        d_up = grad_out * activated
        largest = jnp.maximum(largest, jnp.maximum(peak(d_gate), peak(d_up)))
        both[:, n : n + step] = d_gate.astype(bf16)
        both[:, units + n : units + n + step] = d_up.astype(bf16)

    power = exponent(largest)
    scaled = (both[...].astype(f32) * jnp.exp2(power)).astype(bf16)
    sent_ref[:count, :] = scaled[:, :units]
    sent_ref[count : 2 * count, :] = scaled[:, units:]
    sent_ref[2 * count :, :] = jnp.broadcast_to(power, (EXTRA, units)).astype(bf16)

    turned[...] = both[...].T
    left = lax.broadcasted_iota(jnp.int32, (BLOCK, count), 1) < half

    def backward(g, carry):
        at = pl.ds(pl.multiple_of(g * 2 * BLOCK, BLOCK), 2 * BLOCK)
        back = jnp.exp2(-w_ref[g, 2 * BLOCK + 2 : 2 * BLOCK + 3, :count].astype(f32))
        pair = jnp.dot(full[at, :], turned[...], preferred_element_type=f32) * back
        upper, lower = pair[:BLOCK], pair[BLOCK:]
        first = jnp.where(left, upper, pltpu.roll(lower, half, 1))
        second = jnp.where(left, pltpu.roll(upper, half, 1), lower)
        share_ref[2 * g, :BLOCK, :] = first.astype(bf16)
        share_ref[2 * g + 1, :BLOCK, :] = second.astype(bf16)
        share_ref[2 * g, BLOCK:, :] = block_ref[SPLIT:, :]
        share_ref[2 * g + 1, BLOCK:, :] = block_ref[SPLIT:, :]
        deliver(g).start()
        return carry

    def finish(g, carry):
        deliver(g).wait()
        return carry

    lax.fori_loop(0, groups, backward, 0, unroll=groups)
    lax.fori_loop(0, groups, finish, 0)


def add_up(shares_ref, out_ref):
    half = out_ref.shape[0]
    total = shares_ref[0, :BLOCK, :].astype(f32)
    for i in range(1, shares_ref.shape[0]):
        total = total + shares_ref[i, :BLOCK, :].astype(f32)
    total = total.T
    out_ref[:, :BLOCK] = total[:half].astype(bf16)
    out_ref[:, BLOCK:] = total[half:].astype(bf16)


def weight_gradients(
    both_ref, got_ref, shares_ref, gate_keep, up_keep, gate_ref, up_ref, columns, both, total, sems, out_sems
):
    sources, units = both_ref.shape[0], gate_ref.shape[1]
    count = columns.shape[1] // sources

    def fetch(c):
        return pltpu.make_async_copy(both_ref.at[c], both.at[c], sems.at[c])

    for c in range(sources):
        fetch(c).start()
    part, step = sources // PARTS, 256
    copies = []
    for p in range(PARTS):
        for c in range(p * part, (p + 1) * part):
            fetch(c).wait()
            back = jnp.exp2(-both[c, 2 * count : 2 * count + 1, :BLOCK].astype(f32)).astype(bf16)
            for h in range(2):
                tile = jnp.concatenate(
                    [got_ref[2 * c + h, count:, :], shares_ref[2 * c + h, BLOCK:, :]], axis=0
                )
                columns[h * BLOCK : (h + 1) * BLOCK, c * count : (c + 1) * count] = (tile * back).T
        inner = slice(p * part * count, (p + 1) * part * count)
        for n in range(0, 2 * units, step):
            at, start = slice(n, n + step), n % units
            lines = slice(0, count) if n < units else slice(count, 2 * count)
            right = jnp.concatenate(
                [both[c, lines, start : start + step] for c in range(p * part, (p + 1) * part)],
                axis=0,
            )
            term = jnp.dot(columns[:, inner], right, preferred_element_type=f32)
            if p > 0:
                term = total[:, at] + term
            if p < PARTS - 1:
                total[:, at] = term
                continue
            ref, keep = (gate_ref, gate_keep) if n < units else (up_ref, up_keep)
            for h in range(2):
                for j in range(step // BLOCK):
                    tile = term[h * BLOCK : (h + 1) * BLOCK, j * BLOCK : (j + 1) * BLOCK]
                    mask = keep[h, start // BLOCK + j].astype(f32)
                    column = n + j * BLOCK
                    total[h * BLOCK : (h + 1) * BLOCK, column : column + BLOCK] = tile * mask
            copy = pltpu.make_async_copy(
                total.at[:, pl.ds(n, step)], ref.at[:, pl.ds(start, step)], out_sems.at[n // step]
            )
            copy.start()
            copies.append(copy)
    for copy in copies:
        copy.wait()


def kernel(body, outs, specs, scratch, sems, megabytes, flops):
    spaces = {"v": pltpu.VMEM, "s": pltpu.SMEM, "h": pltpu.HBM}
    places = [pl.BlockSpec(memory_space=spaces[s]) for s in specs]
    return pl.pallas_call(
        body,
        out_shape=[
            pltpu.HBM(shape, dtype) if s == "h" else jax.ShapeDtypeStruct(shape, dtype)
            for s, (shape, dtype) in zip(specs[-len(outs) :], outs)
        ],
        in_specs=places[: -len(outs)],
        out_specs=places[-len(outs) :],
        scratch_shapes=[
            pltpu.VMEM(shape[1:], f32) if shape[0] is f32 else pltpu.VMEM(shape, bf16)
            for shape in scratch
        ]
        + [pltpu.SemaphoreType.DMA((n,)) for n in sems],
        compiler_params=pltpu.CompilerParams(vmem_limit_bytes=megabytes * 2**20),
        cost_estimate=pl.CostEstimate(flops=flops, bytes_accessed=4 * 2**20, transcendentals=0),
    )


def shards(tokens, gate_weight, up_weight, gate_keep, up_keep, cotangent):
    rows, cols = lax.axis_size("row"), lax.axis_size("col")
    count, width = tokens.shape
    units = cotangent.shape[1]

    route = [
        (r * cols + c, (2 * c + r % 2) * cols + r // 2) for r in range(rows) for c in range(cols)
    ]
    block = lax.ppermute(tokens, ("row", "col"), route)

    packed, same = kernel(
        pack,
        [((2 * BLOCK + EXTRA, units), bf16), ((count, width), bf16)],
        "vvvssvv",
        [],
        [],
        8,
        4 * BLOCK * units,
    )(gate_weight, up_weight, tokens, gate_keep, up_keep)
    packed = packed[: 2 * BLOCK + MARKS].astype(f16)

    (copies,) = kernel(
        spread, [((rows, count + SPLIT, width), bf16)], "vvh", [(count + SPLIT, width)], [rows], 48, 1
    )(same, block)
    copies, packed = lax.optimization_barrier((copies, packed))
    got = lax.all_to_all(copies, "row", 0, 0, tiled=True)

    weights = lax.all_gather(packed, "col", axis=0).astype(bf16)

    hidden, sent, share = kernel(
        forward,
        [
            ((count, units), bf16),
            ((2 * count + EXTRA, units), bf16),
            ((rows, BLOCK + count - SPLIT, count), bf16),
        ],
        "vhvvvvh",
        [
            (count, rows * width),
            (rows * width, 2 * units),
            (count, 2 * units),
            (cols, 2 * BLOCK + MARKS, units),
            (rows, BLOCK + count - SPLIT, count),
            (2 * units, count),
            (f32, count, 2 * units),
        ],
        [cols, cols],
        48,
        8 * count * rows * width * units,
    )(got, weights, cotangent, block)

    shares = lax.all_to_all(share, "row", 0, 0, tiled=True)

    both_all = lax.all_gather(sent[: 2 * count + MARKS].astype(f16), "col", axis=0).astype(bf16)

    (total,) = kernel(add_up, [((count // 2, 2 * width), bf16)], "vv", [], [], 48, 10**6)(shares)
    grad_tokens = lax.ppermute(total, ("row", "col"), route)

    grad_gate, grad_up = kernel(
        weight_gradients,
        [((2 * BLOCK, units), f32)] * 2,
        "hvvsshh",
        [(2 * BLOCK, cols * count), (cols, 2 * count + MARKS, units), (f32, 2 * BLOCK, 2 * units)],
        [cols, 4],
        48,
        8 * BLOCK * cols * count * units,
    )(both_all, got, shares, gate_keep, up_keep)
    return hidden, grad_tokens, grad_gate, grad_up


def solution(mesh):
    return jax.shard_map(
        shards,
        mesh=mesh,
        in_specs=(P("col", "row"),) * 6,
        out_specs=(P("col", "row"), P("row", "col"), P("col", "row"), P("col", "row")),
        check_vma=False,
    )
```

```python
import functools

import jax
import jax.numpy as jnp
from jax import lax
from jax.experimental import pallas as pl
from jax.experimental.pallas import tpu as pltpu
from jax.sharding import PartitionSpec as P

BLOCK = 128
EXTRA = 16
MARKS = 8
PARTS = 4
bf16 = jnp.bfloat16
f16 = jnp.float16
f32 = jnp.float32


def exponent(largest):
    return jnp.floor(14.0 - jnp.log2(jnp.maximum(largest, 2.0**-100)))


def peak(values):
    return jnp.max(jnp.max(jnp.abs(values), axis=0, keepdims=True), axis=1, keepdims=True)


def pack(gate_ref, up_ref, tokens_ref, gate_keep, up_keep, packed_ref, same_ref):
    units = gate_ref.shape[1]
    same_ref[...] = tokens_ref[...]
    line = lax.broadcasted_iota(jnp.int32, (EXTRA, BLOCK), 0)
    tiles, marks = [], []
    for ref, keep in ((gate_ref, gate_keep), (up_ref, up_keep)):
        for j in range(units // BLOCK):
            at = slice(j * BLOCK, (j + 1) * BLOCK)
            first = keep[0, j]
            tiles.append(jnp.where(first > 0, ref[:BLOCK, at], ref[BLOCK:, at]).astype(f32))
            marks.append(first.astype(f32))
    largest = functools.reduce(jnp.maximum, [peak(tile) for tile in tiles])
    power = exponent(largest)
    scale = jnp.exp2(power)
    count = units // BLOCK
    for j in range(count):
        at = slice(j * BLOCK, (j + 1) * BLOCK)
        packed_ref[:BLOCK, at] = (tiles[j] * scale).astype(bf16)
        packed_ref[BLOCK : 2 * BLOCK, at] = (tiles[count + j] * scale).astype(bf16)
        lines = jnp.where(line == 0, marks[j], jnp.where(line == 1, marks[count + j], 0.0))
        packed_ref[2 * BLOCK :, at] = jnp.where(line == 2, power, lines).astype(bf16)


def spread(tokens_ref, copies_ref, sems):
    copies = [
        pltpu.make_async_copy(tokens_ref, copies_ref.at[i], sems.at[i]) for i in range(copies_ref.shape[0])
    ]
    for copy in copies:
        copy.start()
    for copy in copies:
        copy.wait()


def forward(
    got_ref, weights_ref, grad_ref, block_ref, hidden_ref, sent_ref, shares_ref,
    rows, full, both, w_ref, share_ref, turned, total, sems, out_sems,
):
    groups, units = weights_ref.shape[0], weights_ref.shape[2]
    count = grad_ref.shape[0]
    half = count // 2

    def fetch(g):
        return pltpu.make_async_copy(weights_ref.at[g], w_ref.at[g], sems.at[g])

    def deliver(g):
        at = pl.ds(2 * g, 2)
        return pltpu.make_async_copy(share_ref.at[at], shares_ref.at[at], out_sems.at[g])

    def begin(g, carry):
        fetch(g).start()
        return carry

    def expand(g, carry):
        at = pl.ds(pl.multiple_of(g * 2 * BLOCK, BLOCK), BLOCK)
        after = pl.ds(pl.multiple_of(g * 2 * BLOCK + BLOCK, BLOCK), BLOCK)
        fetch(g).wait()
        marks = w_ref[g, 2 * BLOCK :, :]
        back = jnp.exp2(-marks[2:3, :BLOCK].astype(f32)).astype(bf16)
        rows[:, at] = got_ref[2 * g, :count, :] * back
        rows[:, after] = got_ref[2 * g + 1, :count, :] * back
        for part in range(2):
            columns = pl.ds(part * units, units)
            tile = w_ref[g, part * BLOCK : (part + 1) * BLOCK, :]
            first = marks[part : part + 1]
            full[at, columns] = tile * first
            full[after, columns] = tile * (1 - first)
        return carry

    lax.fori_loop(0, groups, begin, 0)
    part, step = groups // PARTS, 256
    for p in range(PARTS):
        lax.fori_loop(p * part, (p + 1) * part, expand, 0, unroll=part)
        inner = slice(p * part * 2 * BLOCK, (p + 1) * part * 2 * BLOCK)
        for n in range(0, 2 * units, step):
            at = slice(n, n + step)
            term = jnp.dot(rows[:, inner], full[inner, at], preferred_element_type=f32)
            total[:, at] = term if p == 0 else total[:, at] + term

    largest = jnp.zeros((1, 1), f32)
    for n in range(0, units, step):
        gate, up = total[:, n : n + step], total[:, units + n : units + n + step]
        sigmoid_gate = jax.nn.sigmoid(gate)
        activated = gate * sigmoid_gate
        hidden_ref[:, n : n + step] = (activated * up).astype(bf16)
        grad_out = grad_ref[:, n : n + step].astype(f32)
        d_gate = grad_out * up * sigmoid_gate * (1.0 + gate * (1.0 - sigmoid_gate))
        d_up = grad_out * activated
        largest = jnp.maximum(largest, jnp.maximum(peak(d_gate), peak(d_up)))
        both[:, n : n + step] = d_gate.astype(bf16)
        both[:, units + n : units + n + step] = d_up.astype(bf16)

    power = exponent(largest)
    scaled = (both[...].astype(f32) * jnp.exp2(power)).astype(bf16)
    sent_ref[:count, :] = scaled[:, :units]
    sent_ref[count : 2 * count, :] = scaled[:, units:]
    sent_ref[2 * count :, :] = jnp.broadcast_to(power, (EXTRA, units)).astype(bf16)

    turned[...] = both[...].T
    left = lax.broadcasted_iota(jnp.int32, (BLOCK, count), 1) < half

    def backward(g, carry):
        at = pl.ds(pl.multiple_of(g * 2 * BLOCK, BLOCK), 2 * BLOCK)
        back = jnp.exp2(-w_ref[g, 2 * BLOCK + 2 : 2 * BLOCK + 3, :count].astype(f32))
        pair = jnp.dot(full[at, :], turned[...], preferred_element_type=f32) * back
        upper, lower = pair[:BLOCK], pair[BLOCK:]
        first = jnp.where(left, upper, pltpu.roll(lower, half, 1))
        second = jnp.where(left, pltpu.roll(upper, half, 1), lower)
        share_ref[2 * g, :BLOCK, :] = first.astype(bf16)
        share_ref[2 * g + 1, :BLOCK, :] = second.astype(bf16)
        share_ref[2 * g, BLOCK:, :] = block_ref[...]
        share_ref[2 * g + 1, BLOCK:, :] = block_ref[...]
        deliver(g).start()
        return carry

    def finish(g, carry):
        deliver(g).wait()
        return carry

    lax.fori_loop(0, groups, backward, 0, unroll=groups)
    lax.fori_loop(0, groups, finish, 0)


def add_up(shares_ref, out_ref):
    half = out_ref.shape[0]
    total = shares_ref[0, :BLOCK, :].astype(f32)
    for i in range(1, shares_ref.shape[0]):
        total = total + shares_ref[i, :BLOCK, :].astype(f32)
    total = total.T
    out_ref[:, :BLOCK] = total[:half].astype(bf16)
    out_ref[:, BLOCK:] = total[half:].astype(bf16)


def weight_gradients(
    both_ref, shares_ref, gate_keep, up_keep, gate_ref, up_ref, columns, both, total, sems, out_sems
):
    sources, units = both_ref.shape[0], gate_ref.shape[1]
    count = columns.shape[1] // sources

    def fetch(c):
        return pltpu.make_async_copy(both_ref.at[c], both.at[c], sems.at[c])

    for c in range(sources):
        fetch(c).start()
    part, step = sources // PARTS, 256
    copies = []
    for p in range(PARTS):
        for c in range(p * part, (p + 1) * part):
            fetch(c).wait()
            back = jnp.exp2(-both[c, 2 * count : 2 * count + 1, :BLOCK].astype(f32)).astype(bf16)
            for h in range(2):
                tile = shares_ref[2 * c + h, BLOCK:, :]
                columns[h * BLOCK : (h + 1) * BLOCK, c * count : (c + 1) * count] = (tile * back).T
        inner = slice(p * part * count, (p + 1) * part * count)
        for n in range(0, 2 * units, step):
            at, start = slice(n, n + step), n % units
            lines = slice(0, count) if n < units else slice(count, 2 * count)
            right = jnp.concatenate(
                [both[c, lines, start : start + step] for c in range(p * part, (p + 1) * part)],
                axis=0,
            )
            term = jnp.dot(columns[:, inner], right, preferred_element_type=f32)
            if p > 0:
                term = total[:, at] + term
            if p < PARTS - 1:
                total[:, at] = term
                continue
            ref, keep = (gate_ref, gate_keep) if n < units else (up_ref, up_keep)
            for h in range(2):
                for j in range(step // BLOCK):
                    tile = term[h * BLOCK : (h + 1) * BLOCK, j * BLOCK : (j + 1) * BLOCK]
                    mask = keep[h, start // BLOCK + j].astype(f32)
                    column = n + j * BLOCK
                    total[h * BLOCK : (h + 1) * BLOCK, column : column + BLOCK] = tile * mask
            copy = pltpu.make_async_copy(
                total.at[:, pl.ds(n, step)], ref.at[:, pl.ds(start, step)], out_sems.at[n // step]
            )
            copy.start()
            copies.append(copy)
    for copy in copies:
        copy.wait()


def kernel(body, outs, specs, scratch, sems, megabytes, flops):
    spaces = {"v": pltpu.VMEM, "s": pltpu.SMEM, "h": pltpu.HBM}
    places = [pl.BlockSpec(memory_space=spaces[s]) for s in specs]
    return pl.pallas_call(
        body,
        out_shape=[
            pltpu.HBM(shape, dtype) if s == "h" else jax.ShapeDtypeStruct(shape, dtype)
            for s, (shape, dtype) in zip(specs[-len(outs) :], outs)
        ],
        in_specs=places[: -len(outs)],
        out_specs=places[-len(outs) :],
        scratch_shapes=[
            pltpu.VMEM(shape[1:], f32) if shape[0] is f32 else pltpu.VMEM(shape, bf16)
            for shape in scratch
        ]
        + [pltpu.SemaphoreType.DMA((n,)) for n in sems],
        compiler_params=pltpu.CompilerParams(vmem_limit_bytes=megabytes * 2**20),
        cost_estimate=pl.CostEstimate(flops=flops, bytes_accessed=4 * 2**20, transcendentals=0),
    )


def shards(tokens, gate_weight, up_weight, gate_keep, up_keep, cotangent):
    rows, cols = lax.axis_size("row"), lax.axis_size("col")
    count, width = tokens.shape
    units = cotangent.shape[1]

    route = [
        (r * cols + c, (2 * c + r % 2) * cols + r // 2) for r in range(rows) for c in range(cols)
    ]
    packed, same = kernel(
        pack,
        [((2 * BLOCK + EXTRA, units), bf16), ((count, width), bf16)],
        "vvvssvv",
        [],
        [],
        8,
        4 * BLOCK * units,
    )(gate_weight, up_weight, tokens, gate_keep, up_keep)
    packed = packed[: 2 * BLOCK + MARKS].astype(f16)

    (copies,) = kernel(
        spread, [((rows, count, width), bf16)], "vh", [], [rows], 48, 1
    )(tokens)
    packed, same = lax.optimization_barrier((packed, same))
    block = lax.ppermute(same, ("row", "col"), route)
    got = lax.all_to_all(copies, "row", 0, 0, tiled=True)

    weights = lax.all_gather(packed, "col", axis=0).astype(bf16)

    hidden, sent, share = kernel(
        forward,
        [
            ((count, units), bf16),
            ((2 * count + EXTRA, units), bf16),
            ((rows, BLOCK + count, count), bf16),
        ],
        "vhvvvvh",
        [
            (count, rows * width),
            (rows * width, 2 * units),
            (count, 2 * units),
            (cols, 2 * BLOCK + MARKS, units),
            (rows, BLOCK + count, count),
            (2 * units, count),
            (f32, count, 2 * units),
        ],
        [cols, cols],
        50,
        8 * count * rows * width * units,
    )(got, weights, cotangent, block)

    shares = lax.all_to_all(share, "row", 0, 0, tiled=True)

    both_all = lax.all_gather(sent[: 2 * count + MARKS].astype(f16), "col", axis=0).astype(bf16)

    (total,) = kernel(add_up, [((count // 2, 2 * width), bf16)], "vv", [], [], 48, 10**6)(shares)
    grad_tokens = lax.ppermute(total, ("row", "col"), route)

    grad_gate, grad_up = kernel(
        weight_gradients,
        [((2 * BLOCK, units), f32)] * 2,
        "hvsshh",
        [(2 * BLOCK, cols * count), (cols, 2 * count + MARKS, units), (f32, 2 * BLOCK, 2 * units)],
        [cols, 4],
        48,
        8 * BLOCK * cols * count * units,
    )(both_all, shares, gate_keep, up_keep)
    return hidden, grad_tokens, grad_gate, grad_up


def solution(mesh):
    return jax.shard_map(
        shards,
        mesh=mesh,
        in_specs=(P("col", "row"),) * 6,
        out_specs=(P("col", "row"), P("row", "col"), P("col", "row"), P("col", "row")),
        check_vma=False,
    )
```

```python
import functools

import jax
import jax.numpy as jnp
from jax import lax
from jax.experimental import pallas as pl
from jax.experimental.pallas import tpu as pltpu
from jax.sharding import PartitionSpec as P

BLOCK = 128
EXTRA = 16
MARKS = 8
PARTS = 4
SPLIT = 80
bf16 = jnp.bfloat16
f16 = jnp.float16
f32 = jnp.float32


def exponent(largest):
    return jnp.floor(14.0 - jnp.log2(jnp.maximum(largest, 2.0**-100)))


def peak(values):
    return jnp.max(jnp.max(jnp.abs(values), axis=0, keepdims=True), axis=1, keepdims=True)


def pack(gate_ref, up_ref, tokens_ref, gate_keep, up_keep, packed_ref, same_ref):
    units = gate_ref.shape[1]
    same_ref[...] = tokens_ref[...]
    line = lax.broadcasted_iota(jnp.int32, (EXTRA, BLOCK), 0)
    tiles, marks = [], []
    for ref, keep in ((gate_ref, gate_keep), (up_ref, up_keep)):
        for j in range(units // BLOCK):
            at = slice(j * BLOCK, (j + 1) * BLOCK)
            first = keep[0, j]
            tiles.append(jnp.where(first > 0, ref[:BLOCK, at], ref[BLOCK:, at]).astype(f32))
            marks.append(first.astype(f32))
    largest = functools.reduce(jnp.maximum, [peak(tile) for tile in tiles])
    power = exponent(largest)
    scale = jnp.exp2(power)
    count = units // BLOCK
    for j in range(count):
        at = slice(j * BLOCK, (j + 1) * BLOCK)
        packed_ref[:BLOCK, at] = (tiles[j] * scale).astype(bf16)
        packed_ref[BLOCK : 2 * BLOCK, at] = (tiles[count + j] * scale).astype(bf16)
        lines = jnp.where(line == 0, marks[j], jnp.where(line == 1, marks[count + j], 0.0))
        packed_ref[2 * BLOCK :, at] = jnp.where(line == 2, power, lines).astype(bf16)


def spread(tokens_ref, block_ref, copies_ref, one, sems):
    count = tokens_ref.shape[0]
    one[:count] = tokens_ref[...]
    one[count:] = block_ref[:SPLIT]
    copies = [
        pltpu.make_async_copy(one, copies_ref.at[i], sems.at[i]) for i in range(copies_ref.shape[0])
    ]
    for copy in copies:
        copy.start()
    for copy in copies:
        copy.wait()


def forward(
    got_ref, weights_ref, grad_ref, block_ref, hidden_ref, sent_ref, share_ref,
    rows, full, both, w_ref, turned, total, sems,
):
    groups, units = weights_ref.shape[0], weights_ref.shape[2]
    count = grad_ref.shape[0]
    half = count // 2

    def fetch(g):
        return pltpu.make_async_copy(weights_ref.at[g], w_ref.at[g], sems.at[g])

    def begin(g, carry):
        fetch(g).start()
        return carry

    def expand(g, carry):
        at = pl.ds(pl.multiple_of(g * 2 * BLOCK, BLOCK), BLOCK)
        after = pl.ds(pl.multiple_of(g * 2 * BLOCK + BLOCK, BLOCK), BLOCK)
        fetch(g).wait()
        marks = w_ref[g, 2 * BLOCK :, :]
        back = jnp.exp2(-marks[2:3, :BLOCK].astype(f32)).astype(bf16)
        rows[:, at] = got_ref[2 * g, :count, :] * back
        rows[:, after] = got_ref[2 * g + 1, :count, :] * back
        for part in range(2):
            columns = pl.ds(part * units, units)
            tile = w_ref[g, part * BLOCK : (part + 1) * BLOCK, :]
            first = marks[part : part + 1]
            full[at, columns] = tile * first
            full[after, columns] = tile * (1 - first)
        return carry

    lax.fori_loop(0, groups, begin, 0)
    part, step = groups // PARTS, 256
    for p in range(PARTS):
        lax.fori_loop(p * part, (p + 1) * part, expand, 0, unroll=part)
        inner = slice(p * part * 2 * BLOCK, (p + 1) * part * 2 * BLOCK)
        for n in range(0, 2 * units, step):
            at = slice(n, n + step)
            term = jnp.dot(rows[:, inner], full[inner, at], preferred_element_type=f32)
            total[:, at] = term if p == 0 else total[:, at] + term

    largest = jnp.zeros((1, 1), f32)
    for n in range(0, units, step):
        gate, up = total[:, n : n + step], total[:, units + n : units + n + step]
        sigmoid_gate = jax.nn.sigmoid(gate)
        activated = gate * sigmoid_gate
        hidden_ref[:, n : n + step] = (activated * up).astype(bf16)
        grad_out = grad_ref[:, n : n + step].astype(f32)
        d_gate = grad_out * up * sigmoid_gate * (1.0 + gate * (1.0 - sigmoid_gate))
        d_up = grad_out * activated
        largest = jnp.maximum(largest, jnp.maximum(peak(d_gate), peak(d_up)))
        both[:, n : n + step] = d_gate.astype(bf16)
        both[:, units + n : units + n + step] = d_up.astype(bf16)

    power = exponent(largest)
    scaled = (both[...].astype(f32) * jnp.exp2(power)).astype(bf16)
    sent_ref[:count, :] = scaled[:, :units]
    sent_ref[count : 2 * count, :] = scaled[:, units:]
    sent_ref[2 * count :, :] = jnp.broadcast_to(power, (EXTRA, units)).astype(bf16)

    turned[...] = both[...].T
    left = lax.broadcasted_iota(jnp.int32, (BLOCK, count), 1) < half

    def backward(g, carry):
        at = pl.ds(pl.multiple_of(g * 2 * BLOCK, BLOCK), 2 * BLOCK)
        back = jnp.exp2(-w_ref[g, 2 * BLOCK + 2 : 2 * BLOCK + 3, :count].astype(f32))
        pair = jnp.dot(full[at, :], turned[...], preferred_element_type=f32) * back
        upper, lower = pair[:BLOCK], pair[BLOCK:]
        first = jnp.where(left, upper, pltpu.roll(lower, half, 1))
        second = jnp.where(left, pltpu.roll(upper, half, 1), lower)
        share_ref[2 * g, :BLOCK, :] = first.astype(bf16)
        share_ref[2 * g + 1, :BLOCK, :] = second.astype(bf16)
        share_ref[2 * g, BLOCK:, :] = block_ref[SPLIT:, :]
        share_ref[2 * g + 1, BLOCK:, :] = block_ref[SPLIT:, :]
        return carry

    lax.fori_loop(0, groups, backward, 0, unroll=groups)


def add_up(shares_ref, out_ref):
    half = out_ref.shape[0]
    total = shares_ref[0, :BLOCK, :].astype(f32)
    for i in range(1, shares_ref.shape[0]):
        total = total + shares_ref[i, :BLOCK, :].astype(f32)
    total = total.T
    out_ref[:, :BLOCK] = total[:half].astype(bf16)
    out_ref[:, BLOCK:] = total[half:].astype(bf16)


def weight_gradients(
    both_ref, got_ref, shares_ref, gate_keep, up_keep, gate_ref, up_ref, columns, both, total, sems, out_sems
):
    sources, units = both_ref.shape[0], gate_ref.shape[1]
    count = columns.shape[1] // sources

    def fetch(c):
        return pltpu.make_async_copy(both_ref.at[c], both.at[c], sems.at[c])

    for c in range(sources):
        fetch(c).start()
    part, step = sources // PARTS, 256
    copies = []
    for p in range(PARTS):
        for c in range(p * part, (p + 1) * part):
            fetch(c).wait()
            back = jnp.exp2(-both[c, 2 * count : 2 * count + 1, :BLOCK].astype(f32)).astype(bf16)
            for h in range(2):
                tile = jnp.concatenate(
                    [got_ref[2 * c + h, count:, :], shares_ref[2 * c + h, BLOCK:, :]], axis=0
                )
                columns[h * BLOCK : (h + 1) * BLOCK, c * count : (c + 1) * count] = (tile * back).T
        inner = slice(p * part * count, (p + 1) * part * count)
        for n in range(0, 2 * units, step):
            at, start = slice(n, n + step), n % units
            lines = slice(0, count) if n < units else slice(count, 2 * count)
            right = jnp.concatenate(
                [both[c, lines, start : start + step] for c in range(p * part, (p + 1) * part)],
                axis=0,
            )
            term = jnp.dot(columns[:, inner], right, preferred_element_type=f32)
            if p > 0:
                term = total[:, at] + term
            if p < PARTS - 1:
                total[:, at] = term
                continue
            ref, keep = (gate_ref, gate_keep) if n < units else (up_ref, up_keep)
            for h in range(2):
                for j in range(step // BLOCK):
                    tile = term[h * BLOCK : (h + 1) * BLOCK, j * BLOCK : (j + 1) * BLOCK]
                    mask = keep[h, start // BLOCK + j].astype(f32)
                    column = n + j * BLOCK
                    total[h * BLOCK : (h + 1) * BLOCK, column : column + BLOCK] = tile * mask
            copy = pltpu.make_async_copy(
                total.at[:, pl.ds(n, step)], ref.at[:, pl.ds(start, step)], out_sems.at[n // step]
            )
            copy.start()
            copies.append(copy)
    for copy in copies:
        copy.wait()


def kernel(body, outs, specs, scratch, sems, megabytes, flops):
    spaces = {"v": pltpu.VMEM, "s": pltpu.SMEM, "h": pltpu.HBM}
    places = [pl.BlockSpec(memory_space=spaces[s]) for s in specs]
    return pl.pallas_call(
        body,
        out_shape=[jax.ShapeDtypeStruct(shape, dtype) for shape, dtype in outs],
        in_specs=places[: -len(outs)],
        out_specs=places[-len(outs) :],
        scratch_shapes=[
            pltpu.VMEM(shape[1:], f32) if shape[0] is f32 else pltpu.VMEM(shape, bf16)
            for shape in scratch
        ]
        + [pltpu.SemaphoreType.DMA((n,)) for n in sems],
        compiler_params=pltpu.CompilerParams(vmem_limit_bytes=megabytes * 2**20),
        cost_estimate=pl.CostEstimate(flops=flops, bytes_accessed=4 * 2**20, transcendentals=0),
    )


def shards(tokens, gate_weight, up_weight, gate_keep, up_keep, cotangent):
    rows, cols = lax.axis_size("row"), lax.axis_size("col")
    count, width = tokens.shape
    units = cotangent.shape[1]

    route = [
        (r * cols + c, (2 * c + r % 2) * cols + r // 2) for r in range(rows) for c in range(cols)
    ]
    block = lax.ppermute(tokens, ("row", "col"), route)

    packed, same = kernel(
        pack,
        [((2 * BLOCK + EXTRA, units), bf16), ((count, width), bf16)],
        "vvvssvv",
        [],
        [],
        8,
        4 * BLOCK * units,
    )(gate_weight, up_weight, tokens, gate_keep, up_keep)
    packed = packed[: 2 * BLOCK + MARKS].astype(f16)

    (copies,) = kernel(
        spread, [((rows, count + SPLIT, width), bf16)], "vvh", [(count + SPLIT, width)], [rows], 48, 1
    )(same, block)
    copies, packed = lax.optimization_barrier((copies, packed))
    got = lax.all_to_all(copies, "row", 0, 0, tiled=True)

    weights = lax.all_gather(packed, "col", axis=0).astype(bf16)

    hidden, sent, share = kernel(
        forward,
        [
            ((count, units), bf16),
            ((2 * count + EXTRA, units), bf16),
            ((rows, BLOCK + count - SPLIT, count), bf16),
        ],
        "vhvvvvv",
        [
            (count, rows * width),
            (rows * width, 2 * units),
            (count, 2 * units),
            (cols, 2 * BLOCK + MARKS, units),
            (2 * units, count),
            (f32, count, 2 * units),
        ],
        [cols],
        48,
        8 * count * rows * width * units,
    )(got, weights, cotangent, block)

    shares = lax.all_to_all(share, "row", 0, 0, tiled=True)

    both_all = lax.all_gather(sent[: 2 * count + MARKS].astype(f16), "col", axis=0).astype(bf16)

    (total,) = kernel(add_up, [((count // 2, 2 * width), bf16)], "vv", [], [], 48, 10**6)(shares)
    grad_tokens = lax.ppermute(total, ("row", "col"), route)

    grad_gate, grad_up = kernel(
        weight_gradients,
        [((2 * BLOCK, units), f32)] * 2,
        "hvvsshh",
        [(2 * BLOCK, cols * count), (cols, 2 * count + MARKS, units), (f32, 2 * BLOCK, 2 * units)],
        [cols, 4],
        48,
        8 * BLOCK * cols * count * units,
    )(both_all, got, shares, gate_keep, up_keep)
    return hidden, grad_tokens, grad_gate, grad_up


def solution(mesh):
    return jax.shard_map(
        shards,
        mesh=mesh,
        in_specs=(P("col", "row"),) * 6,
        out_specs=(P("col", "row"), P("row", "col"), P("col", "row"), P("col", "row")),
        check_vma=False,
    )
```
